512 devices in a mesh: patch: 64 (over x, z_lo, core), head: 8 (over z_hi, y).
Axes of the slice: x: 4, y: 4, z: 16 (z_hi: 2, z_lo: 8; z = z_hi * 8 + z_lo), core: 2. Of those that a mesh axis runs over, the one named last changes fastest.
Arguments:
- queries: bfloat16 [4096, 3072], P(('patch', 'head')), may hold values from -8 to 8
- keys: bfloat16 [4096, 3072], P(('patch', 'head')), may hold values from -10 to 10
- values: bfloat16 [4096, 3072], P(('patch', 'head')), may hold values from -6 to 6
- stale_keys: bfloat16 [4096, 3072], P('patch', 'head'), may hold values from -10 to 10
- stale_values: bfloat16 [4096, 3072], P('patch', 'head'), may hold values from -6 to 6
- patch_counts: int32 [64], replicated, may hold values from 1 to 64, 3072 in all
- out_weight: bfloat16 [3072, 3072], P('head'), may hold values from -0.109375 to 0.109375
- out_bias: float32 [3072], replicated, may hold values from -3 to 3
- gate_scale: float32 [3072], replicated, may hold values from 0.5 to 2
Outputs:
- branch_out: bfloat16 [4096, 3072], P(('patch', 'head'))
The draws below stay inside these ranges and needn't reach their ends.
Inputs may be any that keep to these rules, and one draw needn't show every extreme that they name: `patch_counts`: live tokens of each patch; at least one patch is full; they sum to 3 / 4 of 4096.
All inputs are finite; a program needn't handle non-finite values.
Results may differ from the reference program's by a relative error of at most 0.013.
Values may be sent and summed in bfloat16 or wider, within the bound.
A program may use at most 64 MiB of HBM per device.

```python
import math
import jax
import jax.numpy as jnp
import numpy as np
from jax import lax

HEADS = 24
HEAD_DIM = 128
D = 3072
PATCH = 64
PATCHES = 64
TOKENS = 4096
N_PATCH = 64


def draw_queries(key, part):
    key = jax.random.fold_in(key, 3)
    drawn = jnp.clip(jax.random.normal(key, (TOKENS, D), jnp.float32), -6.0, 6.0)
    return drawn.astype(jnp.bfloat16)


def draw_stale_keys(key, part):
    key = jax.random.fold_in(key, 5)
    drawn = jnp.clip(2.5 * jax.random.normal(key, (TOKENS, D), jnp.float32), -10.0, 10.0)
    return drawn.astype(jnp.bfloat16)


def block_levels(key, extent, shards, smallest, largest):
    gain, own = 1.0, jax.random.fold_in(key, 6)
    for dim, shards_of in shards:
        draws = jnp.exp(jax.random.uniform(jax.random.fold_in(own, dim), (shards_of,), jnp.float32, smallest / len(shards), largest / len(shards)))
        gain = gain * jnp.repeat(draws, extent[dim] // shards_of).reshape([-1 if axis == dim else 1 for axis in range(len(extent))])
    return gain


def profile(amount, total, reach, lean):
    weights = [(1 << 20) // math.isqrt(standing ** lean) + 1 for standing in range(2, amount + 1)]
    rest, holding = total - reach - (amount - 1), [1] * (amount - 1)
    while rest > 0:
        movable = [i for i in range(amount - 1) if holding[i] < reach]
        whole, remaining = sum([weights[i] for i in movable]), rest
        for i in movable:
            more = min(reach - holding[i], max(1, remaining * weights[i] // whole), rest)
            holding[i] = holding[i] + more
            rest = rest - more
    return np.array([reach] + holding)


def ragged(rng, count, total, reach, skew):
    if count == 2:
        one = jax.random.randint(rng, (), max(1, total - reach), min(reach, total - 1) + 1)
        return jnp.stack([one, total - one])
    sizes = jnp.asarray(profile(count, total, reach, skew), jnp.int32)
    twos = (count - 1) // 2
    source_of, receiver = sizes[1:1 + 2 * twos:2], sizes[2:2 + 2 * twos:2]
    margin = jnp.minimum(source_of - 1, reach - receiver)
    shifted = jax.random.randint(jax.random.fold_in(rng, 1), (twos,), 0, 1 << 20) % (margin + 1)
    sizes = sizes.at[1:1 + 2 * twos:2].set(source_of - shifted).at[2:2 + 2 * twos:2].set(receiver + shifted)
    return sizes[jax.random.permutation(jax.random.fold_in(rng, 2), count)]


def normal_values(stream_key, shape, deviation, limit, split=(), held_as=jnp.bfloat16):
    entries = jax.random.normal(stream_key, shape, jnp.float32) * deviation
    if len(split) > 0:
        entries = block_levels(stream_key, shape, split, -0.22, 0.18) * entries
    return jnp.clip(entries, min=-limit, max=limit).astype(held_as)


def setup_inputs(seed: int = 0) -> dict:
    seeds = jax.random.split(jax.random.key(seed), 10)
    return {
        "queries": draw_queries(jax.random.fold_in(seeds[9], 71), 0),
        "keys": normal_values(seeds[1], (TOKENS, D), 2.5, 10.0, ((0, 512),)),
        "values": normal_values(seeds[2], (TOKENS, D), 1.0, 6.0, ((0, 512),)),
        "stale_keys": draw_stale_keys(jax.random.fold_in(seeds[9], 71), 0),
        "stale_values": normal_values(seeds[4], (TOKENS, D), 1.0, 6.0, ((0, 64), (1, 8))),
        "patch_counts": ragged(seeds[5], PATCHES, PATCH * N_PATCH * 3 // 4, PATCH, 0).astype(jnp.int32),
        "out_weight": normal_values(seeds[6], (D, D), D ** -0.5, 0.109375, ((0, 8),)),
        "out_bias": normal_values(seeds[7], (D,), 0.5, 3.0, (), jnp.float32),
        "gate_scale": jnp.clip(jnp.exp(jax.random.uniform(seeds[8], (D,), jnp.float32, math.log(0.5), math.log(2.0))), 0.5, 2.0),
    }


def reference(queries, keys, values, stale_keys, stale_values, patch_counts, out_weight, out_bias, gate_scale):
    rows = jnp.arange(TOKENS, dtype=jnp.int32)
    row_counts = jnp.repeat(patch_counts, PATCH)
    live = rows % PATCH < row_counts
    factor = 1.0 / math.sqrt(HEAD_DIM)

    def one_patch(index):
        start = (index * PATCH).astype(jnp.int32)
        q_block = lax.dynamic_slice_in_dim(queries, start, PATCH, 0)
        k_all = lax.dynamic_update_slice_in_dim(stale_keys, lax.dynamic_slice_in_dim(keys, start, PATCH, 0), start, 0)
        v_all = lax.dynamic_update_slice_in_dim(stale_values, lax.dynamic_slice_in_dim(values, start, PATCH, 0), start, 0)
        q_heads = q_block.reshape(PATCH, HEADS, HEAD_DIM).astype(jnp.float32)
        k_heads = k_all.reshape(TOKENS, HEADS, HEAD_DIM).astype(jnp.float32)
        v_heads = v_all.reshape(TOKENS, HEADS, HEAD_DIM).astype(jnp.float32)
        scores = jnp.einsum('qhd,khd->hqk', q_heads, k_heads) * factor
        scores = jnp.where(live[None, None, :], scores, -1e+30)
        top = lax.optimization_barrier(jnp.max(scores, axis=-1, keepdims=True))
        expd = jnp.exp(scores - top)
        total = lax.optimization_barrier(jnp.sum(expd, axis=-1))
        weights = expd.astype(jnp.bfloat16)
        mixed = jnp.einsum('hqk,khd->qhd', weights.astype(jnp.float32), v_heads)
        mixed = mixed / jnp.transpose(total)[:, :, None]
        return mixed.reshape(PATCH, D).astype(jnp.bfloat16)
    attended = lax.map(one_patch, jnp.arange(PATCHES, dtype=jnp.int32)).reshape(TOKENS, D)
    projected = jnp.dot(attended, out_weight, preferred_element_type=jnp.float32) + out_bias.astype(jnp.float32)
    result = jnp.where(live[:, None], gate_scale.astype(jnp.float32)[None, :] * projected, 0.0)
    return result.astype(jnp.bfloat16)
```

```python
import math

import jax
import jax.numpy as jnp
from jax import lax
from jax.experimental import pallas as pl
from jax.experimental.pallas import tpu as pltpu
from jax.sharding import PartitionSpec as P

MESH = pl.DeviceIdType.MESH
F32, BF16 = jnp.float32, jnp.bfloat16
HD = 128
NH = 3
W3 = HD * NH
D = 3072
ROWS = 64
NC = 4
CW = D // NC
LOG2E = 1.4426950408889634
SCALE = LOG2E / math.sqrt(HD)
NEG = -1e30


def flat_rows(ref_value):
    v = ref_value.astype(F32)
    return v.reshape(-1, v.shape[-1]).astype(BF16)


def kernel(
    counts, q_in, k_in, v_in, sk_in, sv_in, w_in, bias, gate, out,
    qall, kb, vb, fresh, wv, psend, precv, ssend, srecv, ys, yr, zs, zr,
    loc, s1q_s, s1q_r, s1f_s, s1f_r, g_s, g_r, kx_s, kx_r, kz_s, kz_r, fx_s, fx_r, pp_s, pp_r, ps_s, ps_r, y_s, y_r, z_s, z_r,
):
    p, hd = lax.axis_index("patch"), lax.axis_index("head")
    x, w, vc = p // 16, (p // 8) % 2, p % 8
    zh, y = hd // 4, hd % 4
    quad = p - vc

    def at_vc(k):
        return quad + lax.rem(vc + k, 8)

    def at_x(k):
        return lax.rem(x + k, 4) * 16 + w * 8 + vc

    p_w = x * 16 + (1 - w) * 8 + vc
    other = (1 - zh) * 4

    def at_y(k):
        return zh * 4 + lax.rem(y + k, 4)

    def over_y(k):
        return other + lax.rem(y + k, 4)

    def cols(h):
        return pl.ds(pl.multiple_of(h * W3, HD), W3)

    sends = []

    def send(src, dst, ss, rs, dp, dh):
        c = pltpu.make_async_remote_copy(src_ref=src, dst_ref=dst, send_sem=ss, recv_sem=rs, device_id=(dp, dh), device_id_type=MESH)
        c.start()
        sends.append(c)

    def arrived(dst, ss, rs):
        pltpu.make_async_remote_copy(src_ref=dst, dst_ref=dst, send_sem=ss, recv_sem=rs, device_id=(p_w, hd), device_id_type=MESH).wait_recv()

    locals_ = [
        pltpu.make_async_copy(q_in.at[:, cols(hd)], qall.at[vc, 0, y], loc.at[0]),
        pltpu.make_async_copy(sk_in, kb.at[0, x], loc.at[1]),
        pltpu.make_async_copy(sv_in, vb.at[0, x], loc.at[2]),
        pltpu.make_async_copy(k_in.at[:, cols(hd)], fresh.at[0, 0, zh, y], loc.at[3]),
        pltpu.make_async_copy(v_in.at[:, cols(hd)], fresh.at[1, 0, zh, y], loc.at[4]),
        pltpu.make_async_copy(w_in, wv, loc.at[5]),
    ]
    for c in locals_:
        c.start()

    barrier = pltpu.get_barrier_semaphore()
    greet = [(p_w, hd)]
    greet += [(p_w, over_y(k)) for k in range(4)]
    greet += [(p, at_y(k)) for k in range(1, 4)]
    greet += [(at_vc(k), hd) for k in range(1, 8)]
    greet += [(at_x(k), hd) for k in range(1, 4)]
    for d in greet:
        pl.semaphore_signal(barrier, inc=1, device_id=d, device_id_type=MESH)
    pl.semaphore_wait(barrier, len(greet))

    for k in range(4):
        h = over_y(k)
        send(q_in.at[:, cols(h)], qall.at[vc, 1, y], s1q_s.at[1, k], s1q_r.at[1, k], p_w, h)
    for k in range(1, 4):
        h = at_y(k)
        send(q_in.at[:, cols(h)], qall.at[vc, 0, y], s1q_s.at[0, k], s1q_r.at[0, k], p, h)
    send(sk_in, kb.at[1, x], kz_s.at[0], kz_r.at[0], p_w, hd)
    send(sv_in, vb.at[1, x], kz_s.at[1], kz_r.at[1], p_w, hd)
    for k in (2, 1, 3):
        send(sk_in, kb.at[0, x], kx_s.at[0, 0, k], kx_r.at[0, 0, k], at_x(k), hd)
        send(sv_in, vb.at[0, x], kx_s.at[0, 1, k], kx_r.at[0, 1, k], at_x(k), hd)
    for i, src in enumerate((k_in, v_in)):
        for k in range(4):
            h = over_y(k)
            send(src.at[:, cols(h)], fresh.at[i, 1, zh, y], s1f_s.at[i, 1, k], s1f_r.at[i, 1, k], p_w, h)
        for k in range(1, 4):
            h = at_y(k)
            send(src.at[:, cols(h)], fresh.at[i, 0, zh, y], s1f_s.at[i, 0, k], s1f_r.at[i, 0, k], p, h)

    locals_[0].wait()
    for k in range(1, 4):
        arrived(qall.at[vc, 0, lax.rem(y + 4 - k, 4)], s1q_s.at[0, k], s1q_r.at[0, k])
    for k in (6, 2, 4, 5, 3, 7, 1):
        send(qall.at[vc, 0], qall.at[vc, 0], g_s.at[0, k], g_r.at[0, k], at_vc(k), hd)
    for k in range(4):
        arrived(qall.at[vc, 1, lax.rem(y + 4 - k, 4)], s1q_s.at[1, k], s1q_r.at[1, k])
    for k in (6, 2, 4, 5, 3, 7, 1):
        send(qall.at[vc, 1], qall.at[vc, 1], g_s.at[1, k], g_r.at[1, k], at_vc(k), hd)

    arrived(kb.at[1, x], kz_s.at[0], kz_r.at[0])
    for k in (2, 1, 3):
        send(kb.at[1, x], kb.at[1, x], kx_s.at[1, 0, k], kx_r.at[1, 0, k], at_x(k), hd)
    arrived(vb.at[1, x], kz_s.at[1], kz_r.at[1])
    for k in (2, 1, 3):
        send(vb.at[1, x], vb.at[1, x], kx_s.at[1, 1, k], kx_r.at[1, 1, k], at_x(k), hd)

    locals_[3].wait()
    locals_[4].wait()
    for i in range(2):
        for k in range(1, 4):
            arrived(fresh.at[i, 0, zh, lax.rem(y + 4 - k, 4)], s1f_s.at[i, 0, k], s1f_r.at[i, 0, k])
        send(fresh.at[i, 0, zh], fresh.at[i, 1, zh], fx_s.at[i, 0], fx_r.at[i, 0], p_w, hd)
    for i in range(2):
        for k in range(4):
            arrived(fresh.at[i, 1, 1 - zh, lax.rem(y + 4 - k, 4)], s1f_s.at[i, 1, k], s1f_r.at[i, 1, k])
        send(fresh.at[i, 1, 1 - zh], fresh.at[i, 0, 1 - zh], fx_s.at[i, 1], fx_r.at[i, 1], p_w, hd)

    lane = lax.broadcasted_iota(jnp.int32, (1, 8 * ROWS), 1)
    limit = jnp.zeros((1, 8 * ROWS), jnp.int32)
    patch_of = jnp.zeros((1, 8 * ROWS), jnp.int32)
    for s in range(2):
        for xx in range(4):
            pp = xx * 16 + (w if s == 0 else 1 - w) * 8 + vc
            here = lane // ROWS == s * 4 + xx
            limit = jnp.where(here, counts[pp], limit)
            patch_of = jnp.where(here, pp, patch_of)
    dead = jnp.where(lane % ROWS < limit, 0.0, NEG)

    lanes = lax.broadcasted_iota(jnp.int32, (ROWS, HD), 1)

    def stats_rows(tops, totals):
        t = jnp.zeros((ROWS, HD), F32)
        for h in range(NH):
            t = jnp.where(lanes == h, tops[h], t)
            t = jnp.where(lanes == 8 + h, totals[h], t)
        return jnp.transpose(t)[:16, :]

    def partial(qv, off):
        tops, totals, accs = [], [], []
        for h in range(NH):
            c = slice(h * HD, (h + 1) * HD)
            kh = kb[:, :, :, c].reshape(8 * ROWS, HD)
            vh = vb[:, :, :, c].reshape(8 * ROWS, HD)
            s = lax.dot_general(qv[:, c], kh, (((1,), (1,)), ((), ())), preferred_element_type=F32) * SCALE + off
            top = jnp.max(s, axis=1, keepdims=True)
            e = jnp.exp2(s - top)
            tops.append(top)
            totals.append(jnp.sum(e, axis=1, keepdims=True))
            accs.append(jnp.dot(e.astype(BF16), vh, preferred_element_type=F32))
        return tops, totals, jnp.concatenate(accs, axis=1)

    locals_[1].wait()
    locals_[2].wait()
    for s in range(2):
        for i, buf in enumerate((kb, vb)):
            for k in range(1, 4):
                arrived(buf.at[s, lax.rem(x + 4 - k, 4)], kx_s.at[s, i, k], kx_r.at[s, i, k])

    for k in (6, 2, 4, 5, 3, 7, 1):
        src = lax.rem(vc + 8 - k, 8)
        for half in range(2):
            arrived(qall.at[src, half], g_s.at[half, k], g_r.at[half, k])
        tops, totals, acc = partial(flat_rows(qall[src]), dead)
        psend[src] = acc.astype(BF16)
        ssend[src, :, 0:ROWS] = stats_rows(tops, totals)
        send(psend.at[src], precv.at[vc], pp_s.at[k], pp_r.at[k], quad + src, hd)
        send(ssend.at[src], srecv.at[vc], ps_s.at[k], ps_r.at[k], quad + src, hd)

    mine = flat_rows(qall[vc])
    upper = lax.broadcasted_iota(jnp.int32, (ROWS, 1), 0) < ROWS // 2
    own_patch = jnp.where(upper, p, p_w)
    off = jnp.where(patch_of == own_patch, NEG, dead)
    tops, totals, acc = partial(mine, off)
    precv[vc] = acc.astype(BF16)
    srecv[vc, :, 0:ROWS] = stats_rows(tops, totals)

    for i in range(2):
        arrived(fresh.at[i, 1, zh], fx_s.at[i, 0], fx_r.at[i, 0])
        arrived(fresh.at[i, 0, 1 - zh], fx_s.at[i, 1], fx_r.at[i, 1])
    lane64 = lax.broadcasted_iota(jnp.int32, (1, ROWS), 1)
    f_tops, f_totals, f_accs = [], [], []
    fk = [flat_rows(fresh[0, b]) for b in range(2)]
    fv = [flat_rows(fresh[1, b]) for b in range(2)]
    for h in range(NH):
        c = slice(h * HD, (h + 1) * HD)
        parts = []
        for b in range(2):
            qb = mine[b * 32:(b + 1) * 32, c]
            s = lax.dot_general(qb, fk[b][:, c], (((1,), (1,)), ((), ())), preferred_element_type=F32) * SCALE
            parts.append(s + jnp.where(lane64 < counts[p if b == 0 else p_w], 0.0, NEG))
        s = jnp.concatenate(parts, axis=0)
        top = jnp.max(s, axis=1, keepdims=True)
        e = jnp.exp2(s - top)
        f_tops.append(top)
        f_totals.append(jnp.sum(e, axis=1, keepdims=True))
        eb = e.astype(BF16)
        f_accs.append(jnp.concatenate(
            [jnp.dot(eb[b * 32:(b + 1) * 32], fv[b][:, c], preferred_element_type=F32) for b in range(2)], axis=0))
    f_stats = stats_rows(f_tops, f_totals)

    for k in (1, 7, 3, 5, 4, 2, 6):
        src = lax.rem(vc + k, 8)
        arrived(precv.at[src], pp_s.at[k], pp_r.at[k])
        arrived(srecv.at[src], ps_s.at[k], ps_r.at[k])
    tt = [srecv[j, 0:8, 0:ROWS] for j in range(8)] + [f_stats[0:8]]
    ll = [srecv[j, 8:16, 0:ROWS] for j in range(8)] + [f_stats[8:16]]
    top = tt[0]
    for t in tt[1:]:
        top = jnp.maximum(top, t)
    fade = [jnp.exp2(t - top) for t in tt]
    total = fade[0] * ll[0]
    for f, l in zip(fade[1:], ll[1:]):
        total += f * l
    valid = lax.broadcasted_iota(jnp.int32, (8, ROWS), 0) < NH
    inv = 1.0 / jnp.where(valid, total, 1.0)
    share = jnp.concatenate([f * inv for f in fade] + [jnp.zeros((HD - 72, ROWS), F32)], axis=0)
    share = jnp.transpose(share)
    heads = []
    for h in range(NH):
        c = slice(h * HD, (h + 1) * HD)
        a = f_accs[h] * share[:, 64 + h:65 + h]
        for j in range(8):
            a += precv[j, :, c].astype(F32) * share[:, j * 8 + h:j * 8 + h + 1]
        heads.append(a)
    attended = jnp.concatenate(heads, axis=1).astype(BF16)

    locals_[5].wait()
    for n in range(NC):
        c = slice(n * CW, (n + 1) * CW)
        proj = jnp.dot(attended, wv[:, c], preferred_element_type=F32).reshape(2, 4, 8, CW).astype(BF16)
        ys[1, :, :, c] = proj[1]
        ys[0, :, :, c] = proj[0]
        for k in (2, 1, 3):
            to = lax.rem(y + k, 4)
            send(ys.at[1, to, :, c], yr.at[1, y, :, c], y_s.at[1, n, k], y_r.at[1, n, k], p, at_y(k))
    for n in range(NC):
        c = slice(n * CW, (n + 1) * CW)
        for k in (2, 1, 3):
            to = lax.rem(y + k, 4)
            send(ys.at[0, to, :, c], yr.at[0, y, :, c], y_s.at[0, n, k], y_r.at[0, n, k], p, at_y(k))

    def sum_y(half, n):
        c = slice(n * CW, (n + 1) * CW)
        a = ys[half, y, :, c].astype(F32)
        for k in (1, 3, 2):
            src = lax.rem(y + 4 - k, 4)
            arrived(yr.at[half, src, :, c], y_s.at[half, n, k], y_r.at[half, n, k])
            a += yr[half, src, :, c].astype(F32)
        return a

    for n in range(NC):
        c = slice(n * CW, (n + 1) * CW)
        zs[:, c] = sum_y(1, n).astype(BF16)
        send(zs.at[:, c], zr.at[:, c], z_s.at[n], z_r.at[n], p_w, other + y)

    slot = hd * 8 + lax.broadcasted_iota(jnp.int32, (8, 1), 0)
    live = slot < counts[p]
    halves = [sum_y(0, n) for n in range(NC)]
    for n in range(NC):
        c = slice(n * CW, (n + 1) * CW)
        arrived(zr.at[:, c], z_s.at[n], z_r.at[n])
        whole = halves[n] + zr[:, c].astype(F32) + bias[:, c]
        out[:, c] = jnp.where(live, gate[:, c] * whole, 0.0).astype(BF16)

    for c in sends:
        c.wait_send()


def on_device(queries, keys, values, stale_keys, stale_values, patch_counts, out_weight, out_bias, gate_scale):
    dma = pltpu.SemaphoreType.DMA
    vm = pltpu.VMEM
    hbm = pl.BlockSpec(memory_space=pl.ANY)
    vmem = pl.BlockSpec(memory_space=pltpu.VMEM)

    def pair(*shape):
        return [dma(shape), dma(shape)]

    return pl.pallas_call(
        kernel,
        out_shape=jax.ShapeDtypeStruct((8, D), BF16),
        in_specs=[pl.BlockSpec(memory_space=pltpu.SMEM)] + [hbm] * 6 + [vmem] * 2,
        out_specs=vmem,
        scratch_shapes=[
            vm((8, 2, 4, 8, W3), BF16),
            vm((2, 4, ROWS, W3), BF16),
            vm((2, 4, ROWS, W3), BF16),
            vm((2, 2, 2, 4, 8, W3), BF16),
            vm((W3, D), BF16),
            vm((8, ROWS, W3), BF16),
            vm((8, ROWS, W3), BF16),
            vm((8, 16, HD), F32),
            vm((8, 16, HD), F32),
            vm((2, 4, 8, D), BF16),
            vm((2, 4, 8, D), BF16),
            vm((8, D), BF16),
            vm((8, D), BF16),
            dma((6,)),
            *pair(2, 4),
            *pair(2, 2, 4),
            *pair(2, 8),
            *pair(2, 2, 4),
            *pair(2),
            *pair(2, 2),
            *pair(8),
            *pair(8),
            *pair(2, NC, 4),
            *pair(NC),
        ],
        compiler_params=pltpu.CompilerParams(collective_id=0, has_side_effects=True, vmem_limit_bytes=40 * 2**20),
        cost_estimate=pl.CostEstimate(flops=600_000_000, bytes_accessed=3_000_000, transcendentals=800_000),
    )(patch_counts, queries, keys, values, stale_keys, stale_values, out_weight, out_bias.reshape(1, D), gate_scale.reshape(1, D))


def solution(mesh):
    in_specs = (
        P(("patch", "head"), None),
        P(("patch", "head"), None),
        P(("patch", "head"), None),
        P("patch", "head"),
        P("patch", "head"),
        P(),
        P("head", None),
        P(),
        P(),
    )
    return jax.shard_map(on_device, mesh=mesh, in_specs=in_specs, out_specs=P(("patch", "head"), None), check_vma=False)
```

```python
import math

import jax
import jax.numpy as jnp
from jax import lax
from jax.experimental import pallas as pl
from jax.experimental.pallas import tpu as pltpu
from jax.sharding import PartitionSpec as P

MESH = pl.DeviceIdType.MESH
F32, BF16 = jnp.float32, jnp.bfloat16
HD = 128
NH = 3
W3 = HD * NH
D = 3072
ROWS = 64
NC = 4
CW = D // NC
LOG2E = 1.4426950408889634
SCALE = LOG2E / math.sqrt(HD)
NEG = -1e30


def flat_rows(ref_value):
    v = ref_value.astype(F32)
    return v.reshape(-1, v.shape[-1]).astype(BF16)


def kernel(
    counts_in, q_in, k_in, v_in, sk_in, sv_in, w_in, bias_in, gate_in, out,
    counts, bias, gate, qall, kb, vb, fresh, wv, psend, precv, ssend, srecv, ys, yr, zs, zr,
    loc, s1q_s, s1q_r, s1f_s, s1f_r, g_s, g_r, kx_s, kx_r, kz_s, kz_r, fx_s, fx_r, pp_s, pp_r, ps_s, ps_r, y_s, y_r, z_s, z_r,
):
    p, hd = lax.axis_index("patch"), lax.axis_index("head")
    x, w, vc = p // 16, (p // 8) % 2, p % 8
    zh, y = hd // 4, hd % 4
    quad = p - vc

    def at_vc(k):
        return quad + lax.rem(vc + k, 8)

    def at_x(k):
        return lax.rem(x + k, 4) * 16 + w * 8 + vc

    p_w = x * 16 + (1 - w) * 8 + vc
    other = (1 - zh) * 4

    def at_y(k):
        return zh * 4 + lax.rem(y + k, 4)

    def over_y(k):
        return other + lax.rem(y + k, 4)

    def cols(h):
        return pl.ds(pl.multiple_of(h * W3, HD), W3)

    sends = []

    def send(src, dst, ss, rs, dp, dh):
        c = pltpu.make_async_remote_copy(src_ref=src, dst_ref=dst, send_sem=ss, recv_sem=rs, device_id=(dp, dh), device_id_type=MESH)
        c.start()
        sends.append(c)

    def arrived(dst, ss, rs):
        pltpu.make_async_remote_copy(src_ref=dst, dst_ref=dst, send_sem=ss, recv_sem=rs, device_id=(p_w, hd), device_id_type=MESH).wait_recv()

    locals_ = [
        pltpu.make_async_copy(q_in.at[:, cols(hd)], qall.at[vc, 0, y], loc.at[0]),
        pltpu.make_async_copy(sk_in, kb.at[0, x], loc.at[1]),
        pltpu.make_async_copy(sv_in, vb.at[0, x], loc.at[2]),
        pltpu.make_async_copy(k_in.at[:, cols(hd)], fresh.at[0, 0, zh, y], loc.at[3]),
        pltpu.make_async_copy(v_in.at[:, cols(hd)], fresh.at[1, 0, zh, y], loc.at[4]),
        pltpu.make_async_copy(counts_in, counts, loc.at[6]),
        pltpu.make_async_copy(bias_in, bias, loc.at[7]),
        pltpu.make_async_copy(gate_in, gate, loc.at[8]),
        pltpu.make_async_copy(w_in, wv, loc.at[5]),
    ]
    for c in locals_:
        c.start()

    barrier = pltpu.get_barrier_semaphore()
    greet = [(p_w, hd)]
    greet += [(p_w, over_y(k)) for k in range(4)]
    greet += [(p, at_y(k)) for k in range(1, 4)]
    greet += [(at_vc(k), hd) for k in range(1, 8)]
    greet += [(at_x(k), hd) for k in range(1, 4)]
    for d in greet:
        pl.semaphore_signal(barrier, inc=1, device_id=d, device_id_type=MESH)
    pl.semaphore_wait(barrier, len(greet))

    for k in range(4):
        h = over_y(k)
        send(q_in.at[:, cols(h)], qall.at[vc, 1, y], s1q_s.at[1, k], s1q_r.at[1, k], p_w, h)
    for k in range(1, 4):
        h = at_y(k)
        send(q_in.at[:, cols(h)], qall.at[vc, 0, y], s1q_s.at[0, k], s1q_r.at[0, k], p, h)
    send(sk_in, kb.at[1, x], kz_s.at[0], kz_r.at[0], p_w, hd)
    send(sv_in, vb.at[1, x], kz_s.at[1], kz_r.at[1], p_w, hd)
    for k in (2, 1, 3):
        send(sk_in, kb.at[0, x], kx_s.at[0, 0, k], kx_r.at[0, 0, k], at_x(k), hd)
        send(sv_in, vb.at[0, x], kx_s.at[0, 1, k], kx_r.at[0, 1, k], at_x(k), hd)
    for i, src in enumerate((k_in, v_in)):
        for k in range(4):
            h = over_y(k)
            send(src.at[:, cols(h)], fresh.at[i, 1, zh, y], s1f_s.at[i, 1, k], s1f_r.at[i, 1, k], p_w, h)
        for k in range(1, 4):
            h = at_y(k)
            send(src.at[:, cols(h)], fresh.at[i, 0, zh, y], s1f_s.at[i, 0, k], s1f_r.at[i, 0, k], p, h)

    locals_[0].wait()
    for k in range(1, 4):
        arrived(qall.at[vc, 0, lax.rem(y + 4 - k, 4)], s1q_s.at[0, k], s1q_r.at[0, k])
    for k in (6, 2, 4, 5, 3, 7, 1):
        send(qall.at[vc, 0], qall.at[vc, 0], g_s.at[0, k], g_r.at[0, k], at_vc(k), hd)
    for k in range(4):
        arrived(qall.at[vc, 1, lax.rem(y + 4 - k, 4)], s1q_s.at[1, k], s1q_r.at[1, k])
    for k in (6, 2, 4, 5, 3, 7, 1):
        send(qall.at[vc, 1], qall.at[vc, 1], g_s.at[1, k], g_r.at[1, k], at_vc(k), hd)

    arrived(kb.at[1, x], kz_s.at[0], kz_r.at[0])
    for k in (2, 1, 3):
        send(kb.at[1, x], kb.at[1, x], kx_s.at[1, 0, k], kx_r.at[1, 0, k], at_x(k), hd)
    arrived(vb.at[1, x], kz_s.at[1], kz_r.at[1])
    for k in (2, 1, 3):
        send(vb.at[1, x], vb.at[1, x], kx_s.at[1, 1, k], kx_r.at[1, 1, k], at_x(k), hd)

    locals_[3].wait()
    locals_[4].wait()
    for i in range(2):
        for k in range(1, 4):
            arrived(fresh.at[i, 0, zh, lax.rem(y + 4 - k, 4)], s1f_s.at[i, 0, k], s1f_r.at[i, 0, k])
        send(fresh.at[i, 0, zh], fresh.at[i, 1, zh], fx_s.at[i, 0], fx_r.at[i, 0], p_w, hd)
    for i in range(2):
        for k in range(4):
            arrived(fresh.at[i, 1, 1 - zh, lax.rem(y + 4 - k, 4)], s1f_s.at[i, 1, k], s1f_r.at[i, 1, k])
        send(fresh.at[i, 1, 1 - zh], fresh.at[i, 0, 1 - zh], fx_s.at[i, 1], fx_r.at[i, 1], p_w, hd)

    locals_[5].wait()
    lane = lax.broadcasted_iota(jnp.int32, (1, 8 * ROWS), 1)
    limit = jnp.zeros((1, 8 * ROWS), jnp.int32)
    patch_of = jnp.zeros((1, 8 * ROWS), jnp.int32)
    for s in range(2):
        for xx in range(4):
            pp = xx * 16 + (w if s == 0 else 1 - w) * 8 + vc
            here = lane // ROWS == s * 4 + xx
            limit = jnp.where(here, counts[pp], limit)
            patch_of = jnp.where(here, pp, patch_of)
    dead = jnp.where(lane % ROWS < limit, 0.0, NEG)

    lanes = lax.broadcasted_iota(jnp.int32, (ROWS, HD), 1)

    def stats_rows(tops, totals):
        t = jnp.zeros((ROWS, HD), F32)
        for h in range(NH):
            t = jnp.where(lanes == h, tops[h], t)
            t = jnp.where(lanes == 8 + h, totals[h], t)
        return jnp.transpose(t)[:16, :]

    def partial(qv, off):
        tops, totals, accs = [], [], []
        for h in range(NH):
            c = slice(h * HD, (h + 1) * HD)
            kh = kb[:, :, :, c].reshape(8 * ROWS, HD)
            vh = vb[:, :, :, c].reshape(8 * ROWS, HD)
            s = lax.dot_general(qv[:, c], kh, (((1,), (1,)), ((), ())), preferred_element_type=F32) * SCALE + off
            top = jnp.max(s, axis=1, keepdims=True)
            e = jnp.exp2(s - top)
            tops.append(top)
            totals.append(jnp.sum(e, axis=1, keepdims=True))
            accs.append(jnp.dot(e.astype(BF16), vh, preferred_element_type=F32))
        return tops, totals, jnp.concatenate(accs, axis=1)

    locals_[1].wait()
    locals_[2].wait()
    for s in range(2):
        for i, buf in enumerate((kb, vb)):
            for k in range(1, 4):
                arrived(buf.at[s, lax.rem(x + 4 - k, 4)], kx_s.at[s, i, k], kx_r.at[s, i, k])

    for k in (6, 2, 4, 5, 3, 7, 1):
        src = lax.rem(vc + 8 - k, 8)
        for half in range(2):
            arrived(qall.at[src, half], g_s.at[half, k], g_r.at[half, k])
        tops, totals, acc = partial(flat_rows(qall[src]), dead)
        psend[src] = acc.astype(BF16)
        ssend[src, :, 0:ROWS] = stats_rows(tops, totals)
        send(psend.at[src], precv.at[vc], pp_s.at[k], pp_r.at[k], quad + src, hd)
        send(ssend.at[src], srecv.at[vc], ps_s.at[k], ps_r.at[k], quad + src, hd)

    mine = flat_rows(qall[vc])
    upper = lax.broadcasted_iota(jnp.int32, (ROWS, 1), 0) < ROWS // 2
    own_patch = jnp.where(upper, p, p_w)
    off = jnp.where(patch_of == own_patch, NEG, dead)
    tops, totals, acc = partial(mine, off)
    precv[vc] = acc.astype(BF16)
    srecv[vc, :, 0:ROWS] = stats_rows(tops, totals)

    for i in range(2):
        arrived(fresh.at[i, 1, zh], fx_s.at[i, 0], fx_r.at[i, 0])
        arrived(fresh.at[i, 0, 1 - zh], fx_s.at[i, 1], fx_r.at[i, 1])
    lane64 = lax.broadcasted_iota(jnp.int32, (1, ROWS), 1)
    f_tops, f_totals, f_accs = [], [], []
    fk = [flat_rows(fresh[0, b]) for b in range(2)]
    fv = [flat_rows(fresh[1, b]) for b in range(2)]
    for h in range(NH):
        c = slice(h * HD, (h + 1) * HD)
        parts = []
        for b in range(2):
            qb = mine[b * 32:(b + 1) * 32, c]
            s = lax.dot_general(qb, fk[b][:, c], (((1,), (1,)), ((), ())), preferred_element_type=F32) * SCALE
            parts.append(s + jnp.where(lane64 < counts[p if b == 0 else p_w], 0.0, NEG))
        s = jnp.concatenate(parts, axis=0)
        top = jnp.max(s, axis=1, keepdims=True)
        e = jnp.exp2(s - top)
        f_tops.append(top)
        f_totals.append(jnp.sum(e, axis=1, keepdims=True))
        eb = e.astype(BF16)
        f_accs.append(jnp.concatenate(
            [jnp.dot(eb[b * 32:(b + 1) * 32], fv[b][:, c], preferred_element_type=F32) for b in range(2)], axis=0))
    f_stats = stats_rows(f_tops, f_totals)

    for k in (1, 7, 3, 5, 4, 2, 6):
        src = lax.rem(vc + k, 8)
        arrived(precv.at[src], pp_s.at[k], pp_r.at[k])
        arrived(srecv.at[src], ps_s.at[k], ps_r.at[k])
    tt = [srecv[j, 0:8, 0:ROWS] for j in range(8)] + [f_stats[0:8]]
    ll = [srecv[j, 8:16, 0:ROWS] for j in range(8)] + [f_stats[8:16]]
    top = tt[0]
    for t in tt[1:]:
        top = jnp.maximum(top, t)
    fade = [jnp.exp2(t - top) for t in tt]
    total = fade[0] * ll[0]
    for f, l in zip(fade[1:], ll[1:]):
        total += f * l
    valid = lax.broadcasted_iota(jnp.int32, (8, ROWS), 0) < NH
    inv = 1.0 / jnp.where(valid, total, 1.0)
    share = jnp.concatenate([f * inv for f in fade] + [jnp.zeros((HD - 72, ROWS), F32)], axis=0)
    share = jnp.transpose(share)
    heads = []
    for h in range(NH):
        c = slice(h * HD, (h + 1) * HD)
        a = f_accs[h] * share[:, 64 + h:65 + h]
        for j in range(8):
            a += precv[j, :, c].astype(F32) * share[:, j * 8 + h:j * 8 + h + 1]
        heads.append(a)
    attended = jnp.concatenate(heads, axis=1).astype(BF16)

    for c in locals_[6:]:
        c.wait()
    for n in range(NC):
        c = slice(n * CW, (n + 1) * CW)
        proj = jnp.dot(attended, wv[:, c], preferred_element_type=F32).reshape(2, 4, 8, CW).astype(BF16)
        ys[1, :, :, c] = proj[1]
        ys[0, :, :, c] = proj[0]
        for k in (2, 1, 3):
            to = lax.rem(y + k, 4)
            send(ys.at[1, to, :, c], yr.at[1, y, :, c], y_s.at[1, n, k], y_r.at[1, n, k], p, at_y(k))
    for n in range(NC):
        c = slice(n * CW, (n + 1) * CW)
        for k in (2, 1, 3):
            to = lax.rem(y + k, 4)
            send(ys.at[0, to, :, c], yr.at[0, y, :, c], y_s.at[0, n, k], y_r.at[0, n, k], p, at_y(k))

    def sum_y(half, n):
        c = slice(n * CW, (n + 1) * CW)
        a = ys[half, y, :, c].astype(F32)
        for k in (1, 3, 2):
            src = lax.rem(y + 4 - k, 4)
            arrived(yr.at[half, src, :, c], y_s.at[half, n, k], y_r.at[half, n, k])
            a += yr[half, src, :, c].astype(F32)
        return a

    for n in range(NC):
        c = slice(n * CW, (n + 1) * CW)
        zs[:, c] = sum_y(1, n).astype(BF16)
        send(zs.at[:, c], zr.at[:, c], z_s.at[n], z_r.at[n], p_w, other + y)

    slot = hd * 8 + lax.broadcasted_iota(jnp.int32, (8, 1), 0)
    live = slot < counts[p]
    halves = [sum_y(0, n) for n in range(NC)]
    for n in range(NC):
        c = slice(n * CW, (n + 1) * CW)
        arrived(zr.at[:, c], z_s.at[n], z_r.at[n])
        whole = halves[n] + zr[:, c].astype(F32) + bias[:, c]
        out[:, c] = jnp.where(live, gate[:, c] * whole, 0.0).astype(BF16)

    for c in sends:
        c.wait_send()


def on_device(queries, keys, values, stale_keys, stale_values, patch_counts, out_weight, out_bias, gate_scale):
    dma = pltpu.SemaphoreType.DMA
    vm = pltpu.VMEM
    hbm = pl.BlockSpec(memory_space=pltpu.HBM)
    vmem = pl.BlockSpec(memory_space=pltpu.VMEM)

    def pair(*shape):
        return [dma(shape), dma(shape)]

    return pl.pallas_call(
        kernel,
        out_shape=jax.ShapeDtypeStruct((8, D), BF16),
        in_specs=[hbm] * 9,
        out_specs=vmem,
        scratch_shapes=[
            pltpu.SMEM((64,), jnp.int32),
            vm((1, D), F32),
            vm((1, D), F32),
            vm((8, 2, 4, 8, W3), BF16),
            vm((2, 4, ROWS, W3), BF16),
            vm((2, 4, ROWS, W3), BF16),
            vm((2, 2, 2, 4, 8, W3), BF16),
            vm((W3, D), BF16),
            vm((8, ROWS, W3), BF16),
            vm((8, ROWS, W3), BF16),
            vm((8, 16, HD), F32),
            vm((8, 16, HD), F32),
            vm((2, 4, 8, D), BF16),
            vm((2, 4, 8, D), BF16),
            vm((8, D), BF16),
            vm((8, D), BF16),
            dma((9,)),
            *pair(2, 4),
            *pair(2, 2, 4),
            *pair(2, 8),
            *pair(2, 2, 4),
            *pair(2),
            *pair(2, 2),
            *pair(8),
            *pair(8),
            *pair(2, NC, 4),
            *pair(NC),
        ],
        compiler_params=pltpu.CompilerParams(collective_id=0, has_side_effects=True, vmem_limit_bytes=60 * 2**20),
        cost_estimate=pl.CostEstimate(flops=600_000_000, bytes_accessed=3_000_000, transcendentals=800_000),
    )(patch_counts, queries, keys, values, stale_keys, stale_values, out_weight, out_bias.reshape(1, D), gate_scale.reshape(1, D))


def solution(mesh):
    in_specs = (
        P(("patch", "head"), None),
        P(("patch", "head"), None),
        P(("patch", "head"), None),
        P("patch", "head"),
        P("patch", "head"),
        P(),
        P("head", None),
        P(),
        P(),
    )
    return jax.shard_map(on_device, mesh=mesh, in_specs=in_specs, out_specs=P(("patch", "head"), None), check_vma=False)
```

```python
import math

import jax
import jax.numpy as jnp
from jax import lax
from jax.experimental import pallas as pl
from jax.experimental.pallas import tpu as pltpu
from jax.sharding import PartitionSpec as P

MESH = pl.DeviceIdType.MESH
F32, BF16 = jnp.float32, jnp.bfloat16
HD = 128
NH = 3
W3 = HD * NH
D = 3072
ROWS = 64
KEYS = 8 * ROWS
QS = 4 * ROWS
NC = 4
CW = D // NC
LOG2E = 1.4426950408889634
SCALE = LOG2E / math.sqrt(HD)
NEG = -1e30


def flat_rows(ref_value):
    v = ref_value.astype(F32)
    return v.reshape(-1, v.shape[-1]).astype(BF16)


def kernel(
    counts_in, q_in, k_in, v_in, sk_in, sv_in, w_in, bias_in, gate_in, out,
    counts, bias, gate, qall, kb, vb, fresh, wv, off, acc, ebuf, psend, precv, ssend, srecv, ys, yr, zs, zr,
    loc, s1q_s, s1q_r, s1f_s, s1f_r, g_s, g_r, kx_s, kx_r, kz_s, kz_r, kc_s, kc_r, fx_s, fx_r, pp_s, pp_r, ps_s, ps_r,
    y_s, y_r, z_s, z_r,
):
    p, hd = lax.axis_index("patch"), lax.axis_index("head")
    x, w, v, core = p // 16, (p // 8) % 2, (p // 2) % 4, p % 2
    zh, y = hd // 4, hd % 4

    def at_v(k):
        return p - v * 2 + lax.rem(v + k, 4) * 2

    def at_x(k):
        return p - x * 16 + lax.rem(x + k, 4) * 16

    def back(i, k):
        return lax.rem(i + 4 - k, 4)

    p_w = p - w * 8 + (1 - w) * 8
    p_c = p - core + (1 - core)
    other = (1 - zh) * 4

    def at_y(k):
        return zh * 4 + lax.rem(y + k, 4)

    def over_y(k):
        return other + lax.rem(y + k, 4)

    def cols(h):
        return pl.ds(pl.multiple_of(h * W3, HD), W3)

    sends = []

    def send(src, dst, ss, rs, dp, dh):
        c = pltpu.make_async_remote_copy(src_ref=src, dst_ref=dst, send_sem=ss, recv_sem=rs, device_id=(dp, dh), device_id_type=MESH)
        c.start()
        sends.append(c)

    def arrived(dst, ss, rs):
        pltpu.make_async_remote_copy(src_ref=dst, dst_ref=dst, send_sem=ss, recv_sem=rs, device_id=(p_w, hd), device_id_type=MESH).wait_recv()

    barrier = pltpu.get_barrier_semaphore()
    greet = [(p_w, hd), (p_c, hd)]
    greet += [(p_w, over_y(k)) for k in range(4)]
    greet += [(p, at_y(k)) for k in range(1, 4)]
    greet += [(at_v(k), hd) for k in range(1, 4)]
    greet += [(at_x(k), hd) for k in range(1, 4)]
    for d in greet:
        pl.semaphore_signal(barrier, inc=1, device_id=d, device_id_type=MESH)

    locals_ = [
        pltpu.make_async_copy(counts_in, counts, loc.at[0]),
        pltpu.make_async_copy(q_in.at[:, cols(hd)], qall.at[v, 0, y], loc.at[1]),
        pltpu.make_async_copy(sk_in, kb.at[0, x, core], loc.at[2]),
        pltpu.make_async_copy(sv_in, vb.at[0, x, core], loc.at[3]),
        pltpu.make_async_copy(k_in.at[:, cols(hd)], fresh.at[0, 0, zh, y], loc.at[4]),
        pltpu.make_async_copy(v_in.at[:, cols(hd)], fresh.at[1, 0, zh, y], loc.at[5]),
        pltpu.make_async_copy(bias_in, bias, loc.at[6]),
        pltpu.make_async_copy(gate_in, gate, loc.at[7]),
        pltpu.make_async_copy(w_in, wv, loc.at[8]),
    ]
    for c in locals_:
        c.start()

    locals_[0].wait()
    lane = lax.broadcasted_iota(jnp.int32, (1, KEYS), 1)
    row = lax.broadcasted_iota(jnp.int32, (QS, 1), 0)
    for s in range(2):
        limit = jnp.zeros((1, KEYS), jnp.int32)
        for i in range(8):
            pp = (i // 2) * 16 + (w if s == 0 else 1 - w) * 8 + v * 2 + i % 2
            limit = jnp.where(lane // ROWS == i, counts[pp], limit)
        dead = jnp.where(lane % ROWS < limit, 0.0, NEG)
        own_rows = (row // 32) == v * 2 + s
        own_keys = (lane // ROWS) == x * 2 + core
        off[s] = jnp.where(own_rows & own_keys, NEG, dead)

    pl.semaphore_wait(barrier, len(greet))

    stale = ((sk_in, kb), (sv_in, vb))
    for i, (src, buf) in enumerate(stale):
        send(src, buf.at[1, x, core], kz_s.at[i], kz_r.at[i], p_w, hd)
    for k in range(4):
        h = over_y(k)
        send(q_in.at[:, cols(h)], qall.at[v, 1, y], s1q_s.at[1, k], s1q_r.at[1, k], p_w, h)
    for k in range(1, 4):
        h = at_y(k)
        send(q_in.at[:, cols(h)], qall.at[v, 0, y], s1q_s.at[0, k], s1q_r.at[0, k], p, h)
    for i, (src, buf) in enumerate(stale):
        for k in (2, 1, 3):
            send(src, buf.at[0, x, core], kx_s.at[0, i, k], kx_r.at[0, i, k], at_x(k), hd)
        send(src, buf.at[0, x, core], kc_s.at[0, i, 0], kc_r.at[0, i, 0], p_c, hd)
    for i, src in enumerate((k_in, v_in)):
        for k in range(4):
            h = over_y(k)
            send(src.at[:, cols(h)], fresh.at[i, 1, zh, y], s1f_s.at[i, 1, k], s1f_r.at[i, 1, k], p_w, h)
        for k in range(1, 4):
            h = at_y(k)
            send(src.at[:, cols(h)], fresh.at[i, 0, zh, y], s1f_s.at[i, 0, k], s1f_r.at[i, 0, k], p, h)

    locals_[1].wait()
    for k in range(1, 4):
        arrived(qall.at[v, 0, back(y, k)], s1q_s.at[0, k], s1q_r.at[0, k])
    for k in (2, 1, 3):
        send(qall.at[v, 0], qall.at[v, 0], g_s.at[0, k], g_r.at[0, k], at_v(k), hd)
    for k in range(4):
        arrived(qall.at[v, 1, back(y, k)], s1q_s.at[1, k], s1q_r.at[1, k])
    for k in (2, 1, 3):
        send(qall.at[v, 1], qall.at[v, 1], g_s.at[1, k], g_r.at[1, k], at_v(k), hd)

    def to_core(s, i, k):
        buf = stale[i][1]
        src = back(x, k)
        arrived(buf.at[s, src, core], kx_s.at[s, i, k], kx_r.at[s, i, k])
        send(buf.at[s, src, core], buf.at[s, src, core], kc_s.at[s, i, k], kc_r.at[s, i, k], p_c, hd)

    def from_core(s, i):
        buf = stale[i][1]
        for k in range(4):
            arrived(buf.at[s, back(x, k), 1 - core], kc_s.at[s, i, k], kc_r.at[s, i, k])

    def from_w(i):
        buf = stale[i][1]
        here = buf.at[1, x, core]
        arrived(here, kz_s.at[i], kz_r.at[i])
        for k in (2, 1, 3):
            send(here, here, kx_s.at[1, i, k], kx_r.at[1, i, k], at_x(k), hd)
        send(here, here, kc_s.at[1, i, 0], kc_r.at[1, i, 0], p_c, hd)

    for i in range(2):
        for k in (1, 3, 2):
            to_core(0, i, k)
    from_w(0)
    from_w(1)

    locals_[4].wait()
    locals_[5].wait()
    for i in range(2):
        for k in range(1, 4):
            arrived(fresh.at[i, 0, zh, back(y, k)], s1f_s.at[i, 0, k], s1f_r.at[i, 0, k])
        send(fresh.at[i, 0, zh], fresh.at[i, 1, zh], fx_s.at[i, 0], fx_r.at[i, 0], p_w, hd)
    for i in range(2):
        for k in range(4):
            arrived(fresh.at[i, 1, 1 - zh, back(y, k)], s1f_s.at[i, 1, k], s1f_r.at[i, 1, k])
        send(fresh.at[i, 1, 1 - zh], fresh.at[i, 0, 1 - zh], fx_s.at[i, 1], fx_r.at[i, 1], p_w, hd)

    lanes = lax.broadcasted_iota(jnp.int32, (ROWS, HD), 1)

    def stats_rows(tops, totals):
        t = jnp.zeros((ROWS, HD), F32)
        for h in range(NH):
            t = jnp.where(lanes == h, tops[h], t)
            t = jnp.where(lanes == 8 + h, totals[h], t)
        return jnp.transpose(t)[:16, :]

    def head(h):
        return slice(h * HD, (h + 1) * HD)

    def scores(s, h):
        kh = kb[s, :, :, :, head(h)].reshape(KEYS, HD)
        qk = lax.dot_general(queries[:, head(h)], kh, (((1,), (1,)), ((), ())), preferred_element_type=F32)
        return qk * SCALE + off[s]

    for half in range(2):
        for k in range(1, 4):
            arrived(qall.at[back(v, k), half], g_s.at[half, k], g_r.at[half, k])
    queries = flat_rows(qall[...])
    locals_[2].wait()
    locals_[3].wait()
    from_core(0, 0)
    from_core(0, 1)
    tops, totals = [], []
    for h in range(NH):
        s = scores(0, h)
        top = jnp.max(s, axis=1, keepdims=True)
        e = jnp.exp2(s - top)
        tops.append(top)
        totals.append(jnp.sum(e, axis=1, keepdims=True))
        acc[h] = jnp.dot(e.astype(BF16), vb[0, :, :, :, head(h)].reshape(KEYS, HD), preferred_element_type=F32)

    for k in (1, 3, 2):
        to_core(1, 0, k)
    from_core(1, 0)
    for h in range(NH):
        s = scores(1, h)
        top = jnp.maximum(tops[h], jnp.max(s, axis=1, keepdims=True))
        fade = jnp.exp2(tops[h] - top)
        e = jnp.exp2(s - top)
        tops[h] = top
        totals[h] = totals[h] * fade + jnp.sum(e, axis=1, keepdims=True)
        ebuf[h] = e.astype(BF16)
        acc[h] = acc[h] * fade
    for j in range(4):
        r = slice(j * ROWS, (j + 1) * ROWS)
        ssend[j, :, 0:ROWS] = stats_rows([t[r] for t in tops], [t[r] for t in totals])
    for k in (1, 3, 2):
        to_core(1, 1, k)
    from_core(1, 1)
    for h in range(NH):
        a = acc[h] + jnp.dot(ebuf[h], vb[1, :, :, :, head(h)].reshape(KEYS, HD), preferred_element_type=F32)
        psend[:, :, head(h)] = a.astype(BF16).reshape(4, ROWS, HD)
    for k in (2, 1, 3):
        to = lax.rem(v + k, 4)
        send(psend.at[to], precv.at[v], pp_s.at[k], pp_r.at[k], at_v(k), hd)
        send(ssend.at[to], srecv.at[v], ps_s.at[k], ps_r.at[k], at_v(k), hd)
    precv[v] = psend[v]
    srecv[v] = ssend[v]

    for i in range(2):
        arrived(fresh.at[i, 1, zh], fx_s.at[i, 0], fx_r.at[i, 0])
        arrived(fresh.at[i, 0, 1 - zh], fx_s.at[i, 1], fx_r.at[i, 1])
    mine = flat_rows(qall[v])
    lane64 = lax.broadcasted_iota(jnp.int32, (1, ROWS), 1)
    f_tops, f_totals, f_accs = [], [], []
    fk = [flat_rows(fresh[0, b]) for b in range(2)]
    fv = [flat_rows(fresh[1, b]) for b in range(2)]
    for h in range(NH):
        parts = []
        for b in range(2):
            qb = mine[b * 32:(b + 1) * 32, head(h)]
            s = lax.dot_general(qb, fk[b][:, head(h)], (((1,), (1,)), ((), ())), preferred_element_type=F32) * SCALE
            parts.append(s + jnp.where(lane64 < counts[p if b == 0 else p_w], 0.0, NEG))
        s = jnp.concatenate(parts, axis=0)
        top = jnp.max(s, axis=1, keepdims=True)
        e = jnp.exp2(s - top)
        f_tops.append(top)
        f_totals.append(jnp.sum(e, axis=1, keepdims=True))
        eb = e.astype(BF16)
        f_accs.append(jnp.concatenate(
            [jnp.dot(eb[b * 32:(b + 1) * 32], fv[b][:, head(h)], preferred_element_type=F32) for b in range(2)], axis=0))
    f_stats = stats_rows(f_tops, f_totals)

    for k in (1, 3, 2):
        src = back(v, k)
        arrived(srecv.at[src], ps_s.at[k], ps_r.at[k])
    tt = [srecv[j, 0:8, 0:ROWS] for j in range(4)] + [f_stats[0:8]]
    ll = [srecv[j, 8:16, 0:ROWS] for j in range(4)] + [f_stats[8:16]]
    top = tt[0]
    for t in tt[1:]:
        top = jnp.maximum(top, t)
    fade = [jnp.exp2(t - top) for t in tt]
    total = fade[0] * ll[0]
    for f, l in zip(fade[1:], ll[1:]):
        total += f * l
    valid = lax.broadcasted_iota(jnp.int32, (8, ROWS), 0) < NH
    inv = 1.0 / jnp.where(valid, total, 1.0)
    share = jnp.concatenate([f * inv for f in fade] + [jnp.zeros((HD - 40, ROWS), F32)], axis=0)
    share = jnp.transpose(share)
    for k in (1, 3, 2):
        arrived(precv.at[back(v, k)], pp_s.at[k], pp_r.at[k])
    heads = []
    for h in range(NH):
        a = f_accs[h] * share[:, 32 + h:33 + h]
        for j in range(4):
            a += precv[j, :, head(h)].astype(F32) * share[:, j * 8 + h:j * 8 + h + 1]
        heads.append(a)
    attended = jnp.concatenate(heads, axis=1).astype(BF16)

    for c in locals_[6:]:
        c.wait()
    for n in range(NC):
        c = slice(n * CW, (n + 1) * CW)
        proj = jnp.dot(attended, wv[:, c], preferred_element_type=F32).reshape(2, 4, 8, CW).astype(BF16)
        ys[1, :, :, c] = proj[1]
        ys[0, :, :, c] = proj[0]
        for k in (2, 1, 3):
            to = lax.rem(y + k, 4)
            send(ys.at[1, to, :, c], yr.at[1, y, :, c], y_s.at[1, n, k], y_r.at[1, n, k], p, at_y(k))
    for n in range(NC):
        c = slice(n * CW, (n + 1) * CW)
        for k in (2, 1, 3):
            to = lax.rem(y + k, 4)
            send(ys.at[0, to, :, c], yr.at[0, y, :, c], y_s.at[0, n, k], y_r.at[0, n, k], p, at_y(k))

    def sum_y(half, n):
        c = slice(n * CW, (n + 1) * CW)
        a = ys[half, y, :, c].astype(F32)
        for k in (1, 3, 2):
            src = lax.rem(y + 4 - k, 4)
            arrived(yr.at[half, src, :, c], y_s.at[half, n, k], y_r.at[half, n, k])
            a += yr[half, src, :, c].astype(F32)
        return a

    for n in range(NC):
        c = slice(n * CW, (n + 1) * CW)
        zs[:, c] = sum_y(1, n).astype(BF16)
        send(zs.at[:, c], zr.at[:, c], z_s.at[n], z_r.at[n], p_w, other + y)

    slot = hd * 8 + lax.broadcasted_iota(jnp.int32, (8, 1), 0)
    live = slot < counts[p]
    halves = [sum_y(0, n) for n in range(NC)]
    for n in range(NC):
        c = slice(n * CW, (n + 1) * CW)
        arrived(zr.at[:, c], z_s.at[n], z_r.at[n])
        whole = halves[n] + zr[:, c].astype(F32) + bias[:, c]
        out[:, c] = jnp.where(live, gate[:, c] * whole, 0.0).astype(BF16)

    for c in sends:
        c.wait_send()


def on_device(queries, keys, values, stale_keys, stale_values, patch_counts, out_weight, out_bias, gate_scale):
    dma = pltpu.SemaphoreType.DMA
    vm = pltpu.VMEM
    hbm = pl.BlockSpec(memory_space=pltpu.HBM)
    vmem = pl.BlockSpec(memory_space=pltpu.VMEM)

    def pair(*shape):
        return [dma(shape), dma(shape)]

    return pl.pallas_call(
        kernel,
        out_shape=jax.ShapeDtypeStruct((8, D), BF16),
        in_specs=[hbm] * 9,
        out_specs=vmem,
        scratch_shapes=[
            pltpu.SMEM((64,), jnp.int32),
            vm((1, D), F32),
            vm((1, D), F32),
            vm((4, 2, 4, 8, W3), BF16),
            vm((2, 4, 2, ROWS, W3), BF16),
            vm((2, 4, 2, ROWS, W3), BF16),
            vm((2, 2, 2, 4, 8, W3), BF16),
            vm((W3, D), BF16),
            vm((2, QS, KEYS), F32),
            vm((NH, QS, HD), F32),
            vm((NH, QS, KEYS), BF16),
            vm((4, ROWS, W3), BF16),
            vm((4, ROWS, W3), BF16),
            vm((4, 16, HD), F32),
            vm((4, 16, HD), F32),
            vm((2, 4, 8, D), BF16),
            vm((2, 4, 8, D), BF16),
            vm((8, D), BF16),
            vm((8, D), BF16),
            dma((9,)),
            *pair(2, 4),
            *pair(2, 2, 4),
            *pair(2, 4),
            *pair(2, 2, 4),
            *pair(2),
            *pair(2, 2, 4),
            *pair(2, 2),
            *pair(4),
            *pair(4),
            *pair(2, NC, 4),
            *pair(NC),
        ],
        compiler_params=pltpu.CompilerParams(collective_id=0, has_side_effects=True, vmem_limit_bytes=60 * 2**20),
        cost_estimate=pl.CostEstimate(flops=600_000_000, bytes_accessed=3_000_000, transcendentals=800_000),
    )(patch_counts, queries, keys, values, stale_keys, stale_values, out_weight, out_bias.reshape(1, D), gate_scale.reshape(1, D))


def solution(mesh):
    in_specs = (
        P(("patch", "head"), None),
        P(("patch", "head"), None),
        P(("patch", "head"), None),
        P("patch", "head"),
        P("patch", "head"),
        P(),
        P("head", None),
        P(),
        P(),
    )
    return jax.shard_map(on_device, mesh=mesh, in_specs=in_specs, out_specs=P(("patch", "head"), None), check_vma=False)
```

```python
import math

import jax
import jax.numpy as jnp
from jax import lax
from jax.experimental import pallas as pl
from jax.experimental.pallas import tpu as pltpu
from jax.sharding import PartitionSpec as P

MESH = pl.DeviceIdType.MESH
F32, BF16 = jnp.float32, jnp.bfloat16
HD = 128
NH = 3
W3 = HD * NH
D = 3072
ROWS = 64
KEYS = 8 * ROWS
QS = 4 * ROWS
NC = 4
CW = D // NC
LOG2E = 1.4426950408889634
SCALE = LOG2E / math.sqrt(HD)
NEG = -1e30


def flat_rows(ref_value):
    v = ref_value.astype(F32)
    return v.reshape(-1, v.shape[-1]).astype(BF16)


def kernel(
    counts_in, q_in, k_in, v_in, sk_in, sv_in, w_in, bias_in, gate_in, out,
    counts, bias, gate, qall, k0, v0, k1, v1, fresh, wv, off, acc, ebuf, psend, precv, ssend, srecv, ys, yr, zs, zr, oq, okv,
    loc, s1q_s, s1q_r, s1f_s, s1f_r, g_s, g_r, kx_s, kx_r, kz_s, kz_r, kc_s, kc_r, x1_s, x1_r, c1_s, c1_r, fx_s, fx_r,
    pp_s, pp_r, ps_s, ps_r, y_s, y_r, z_s, z_r,
):
    p, hd = lax.axis_index("patch"), lax.axis_index("head")
    x, w, v, core = p // 16, (p // 8) % 2, (p // 2) % 4, p % 2
    zh, y = hd // 4, hd % 4

    def at_v(k):
        return p - v * 2 + lax.rem(v + k, 4) * 2

    def at_x(k):
        return p - x * 16 + lax.rem(x + k, 4) * 16

    def back(i, k):
        return lax.rem(i + 4 - k, 4)

    p_w = p - w * 8 + (1 - w) * 8
    p_c = p - core + (1 - core)
    other = (1 - zh) * 4

    def at_y(k):
        return zh * 4 + lax.rem(y + k, 4)

    def cols(h):
        return pl.ds(pl.multiple_of(h * W3, HD), W3)

    sends = []

    def send(src, dst, ss, rs, dp, dh):
        c = pltpu.make_async_remote_copy(src_ref=src, dst_ref=dst, send_sem=ss, recv_sem=rs, device_id=(dp, dh), device_id_type=MESH)
        c.start()
        sends.append(c)

    def arrived(dst, ss, rs):
        pltpu.make_async_remote_copy(src_ref=dst, dst_ref=dst, send_sem=ss, recv_sem=rs, device_id=(p_w, hd), device_id_type=MESH).wait_recv()

    barrier = pltpu.get_barrier_semaphore()
    greet = [(p_w, hd), (p_w, other + y), (p_c, hd)]
    greet += [(p, at_y(k)) for k in range(1, 4)]
    greet += [(at_v(k), hd) for k in range(1, 4)]
    greet += [(at_x(k), hd) for k in range(1, 4)]
    for d in greet:
        pl.semaphore_signal(barrier, inc=1, device_id=d, device_id_type=MESH)

    locals_ = [
        pltpu.make_async_copy(q_in.at[:, cols(hd)], qall.at[v, 0, y], loc.at[0]),
        pltpu.make_async_copy(q_in.at[:, cols(other + y)], oq.at[y], loc.at[1]),
        pltpu.make_async_copy(sk_in, k0.at[x, core], loc.at[2]),
        pltpu.make_async_copy(sv_in, v0.at[x, core], loc.at[3]),
        pltpu.make_async_copy(k_in.at[:, cols(hd)], fresh.at[0, 0, zh, y], loc.at[4]),
        pltpu.make_async_copy(v_in.at[:, cols(hd)], fresh.at[1, 0, zh, y], loc.at[5]),
        pltpu.make_async_copy(k_in.at[:, cols(other + y)], okv.at[0, y], loc.at[6]),
        pltpu.make_async_copy(v_in.at[:, cols(other + y)], okv.at[1, y], loc.at[7]),
        pltpu.make_async_copy(counts_in, counts, loc.at[8]),
        pltpu.make_async_copy(bias_in, bias, loc.at[9]),
        pltpu.make_async_copy(gate_in, gate, loc.at[10]),
        pltpu.make_async_copy(w_in, wv, loc.at[11]),
    ]

    def head(h):
        return slice(h * HD, (h + 1) * HD)

    pl.semaphore_wait(barrier, len(greet))

    stale = ((sk_in, k0, k1), (sv_in, v0, v1))
    for i, (src, unused, buf) in enumerate(stale):
        for h in range(NH):
            send(src.at[:, head(h)], buf.at[h, x, core], kz_s.at[i, h], kz_r.at[i, h], p_w, hd)
    for k in (2, 1, 3):
        to = lax.rem(y + k, 4)
        send(q_in.at[:, cols(other + to)], oq.at[y], s1q_s.at[1, k], s1q_r.at[1, k], p, at_y(k))
    for k in (2, 1, 3):
        send(q_in.at[:, cols(at_y(k))], qall.at[v, 0, y], s1q_s.at[0, k], s1q_r.at[0, k], p, at_y(k))
    for i, (src, buf, unused) in enumerate(stale):
        for k in (2, 1, 3):
            send(src, buf.at[x, core], kx_s.at[i, k], kx_r.at[i, k], at_x(k), hd)
        send(src, buf.at[x, core], kc_s.at[i, 0], kc_r.at[i, 0], p_c, hd)
    for c in locals_:
        c.start()
    for i, src in enumerate((k_in, v_in)):
        for k in (2, 1, 3):
            to = lax.rem(y + k, 4)
            send(src.at[:, cols(other + to)], okv.at[i, y], s1f_s.at[i, 1, k], s1f_r.at[i, 1, k], p, at_y(k))
            send(src.at[:, cols(at_y(k))], fresh.at[i, 0, zh, y], s1f_s.at[i, 0, k], s1f_r.at[i, 0, k], p, at_y(k))

    locals_[1].wait()
    for k in (1, 3, 2):
        arrived(oq.at[back(y, k)], s1q_s.at[1, k], s1q_r.at[1, k])
    send(oq, qall.at[v, 1], s1q_s.at[1, 0], s1q_r.at[1, 0], p_w, other + y)
    locals_[0].wait()
    for k in (1, 3, 2):
        arrived(qall.at[v, 0, back(y, k)], s1q_s.at[0, k], s1q_r.at[0, k])
    for k in (2, 1, 3):
        send(qall.at[v, 0], qall.at[v, 0], g_s.at[0, k], g_r.at[0, k], at_v(k), hd)
    for i in range(2):
        locals_[6 + i].wait()
        for k in (1, 3, 2):
            arrived(okv.at[i, back(y, k)], s1f_s.at[i, 1, k], s1f_r.at[i, 1, k])
        send(okv.at[i], fresh.at[i, 1, zh], s1f_s.at[i, 1, 0], s1f_r.at[i, 1, 0], p_w, other + y)

    locals_[8].wait()
    lane = lax.broadcasted_iota(jnp.int32, (1, KEYS), 1)
    row = lax.broadcasted_iota(jnp.int32, (QS, 1), 0)
    for s in range(2):
        limit = jnp.zeros((1, KEYS), jnp.int32)
        for i in range(8):
            pp = (i // 2) * 16 + (w if s == 0 else 1 - w) * 8 + v * 2 + i % 2
            limit = jnp.where(lane // ROWS == i, counts[pp], limit)
        dead = jnp.where(lane % ROWS < limit, 0.0, NEG)
        own_rows = (row // 32) == v * 2 + s
        own_keys = (lane // ROWS) == x * 2 + core
        off[s] = jnp.where(own_rows & own_keys, NEG, dead)

    for i in range(2):
        buf = stale[i][1]
        for k in (1, 3, 2):
            here = buf.at[back(x, k), core]
            arrived(here, kx_s.at[i, k], kx_r.at[i, k])
            send(here, here, kc_s.at[i, k], kc_r.at[i, k], p_c, hd)

    def from_w(i, h):
        here = stale[i][2].at[h, x, core]
        arrived(here, kz_s.at[i, h], kz_r.at[i, h])
        for k in (2, 1, 3):
            send(here, here, x1_s.at[i, h, k], x1_r.at[i, h, k], at_x(k), hd)
        send(here, here, c1_s.at[i, h, 0], c1_r.at[i, h, 0], p_c, hd)

    def to_core(i, h):
        for k in (1, 3, 2):
            here = stale[i][2].at[h, back(x, k), core]
            arrived(here, x1_s.at[i, h, k], x1_r.at[i, h, k])
            send(here, here, c1_s.at[i, h, k], c1_r.at[i, h, k], p_c, hd)

    def from_core(i, h):
        for k in range(4):
            arrived(stale[i][2].at[h, back(x, k), 1 - core], c1_s.at[i, h, k], c1_r.at[i, h, k])

    for h in range(NH):
        from_w(0, h)
    arrived(qall.at[v, 1], s1q_s.at[1, 0], s1q_r.at[1, 0])
    for k in (2, 1, 3):
        send(qall.at[v, 1], qall.at[v, 1], g_s.at[1, k], g_r.at[1, k], at_v(k), hd)
    for i in range(2):
        locals_[4 + i].wait()
        for k in (1, 3, 2):
            arrived(fresh.at[i, 0, zh, back(y, k)], s1f_s.at[i, 0, k], s1f_r.at[i, 0, k])
        send(fresh.at[i, 0, zh], fresh.at[i, 1, zh], fx_s.at[i, 0], fx_r.at[i, 0], p_w, hd)
    for h in range(NH):
        from_w(1, h)
        to_core(0, h)
    for i in range(2):
        arrived(fresh.at[i, 1, 1 - zh], s1f_s.at[i, 1, 0], s1f_r.at[i, 1, 0])
        send(fresh.at[i, 1, 1 - zh], fresh.at[i, 0, 1 - zh], fx_s.at[i, 1], fx_r.at[i, 1], p_w, hd)

    lanes = lax.broadcasted_iota(jnp.int32, (ROWS, HD), 1)

    def stats_rows(tops, totals):
        t = jnp.zeros((ROWS, HD), F32)
        for h in range(NH):
            t = jnp.where(lanes == h, tops[h], t)
            t = jnp.where(lanes == 8 + h, totals[h], t)
        return jnp.transpose(t)[:16, :]

    def weigh(s, h, keys):
        qk = lax.dot_general(queries[:, head(h)], keys, (((1,), (1,)), ((), ())), preferred_element_type=F32)
        return qk * SCALE + off[s]

    for half in range(2):
        for k in (1, 3, 2):
            arrived(qall.at[back(v, k), half], g_s.at[half, k], g_r.at[half, k])
    queries = flat_rows(qall[...])
    for i in range(2):
        locals_[2 + i].wait()
        for k in range(4):
            arrived(stale[i][1].at[back(x, k), 1 - core], kc_s.at[i, k], kc_r.at[i, k])
    tops, totals = [], []
    for h in range(NH):
        s = weigh(0, h, k0[:, :, :, head(h)].reshape(KEYS, HD))
        top = jnp.max(s, axis=1, keepdims=True)
        e = jnp.exp2(s - top)
        tops.append(top)
        totals.append(jnp.sum(e, axis=1, keepdims=True))
        acc[h] = jnp.dot(e.astype(BF16), v0[:, :, :, head(h)].reshape(KEYS, HD), preferred_element_type=F32)
    to_core(1, 0)

    for h in range(NH):
        from_core(0, h)
        s = weigh(1, h, k1[h].reshape(KEYS, HD))
        top = jnp.maximum(tops[h], jnp.max(s, axis=1, keepdims=True))
        fade = jnp.exp2(tops[h] - top)
        e = jnp.exp2(s - top)
        tops[h] = top
        totals[h] = totals[h] * fade + jnp.sum(e, axis=1, keepdims=True)
        ebuf[h] = e.astype(BF16)
        acc[h] = acc[h] * fade
    for j in range(4):
        r = slice(j * ROWS, (j + 1) * ROWS)
        ssend[j, :, 0:ROWS] = stats_rows([t[r] for t in tops], [t[r] for t in totals])
    for k in (2, 1, 3):
        to = lax.rem(v + k, 4)
        send(ssend.at[to], srecv.at[v], ps_s.at[k], ps_r.at[k], at_v(k), hd)
    srecv[v] = ssend[v]
    to_core(1, 1)
    to_core(1, 2)
    for h in range(NH):
        from_core(1, h)
        a = acc[h] + jnp.dot(ebuf[h], v1[h].reshape(KEYS, HD), preferred_element_type=F32)
        psend[h] = a.astype(BF16).reshape(4, ROWS, HD)
        for k in (2, 1, 3):
            to = lax.rem(v + k, 4)
            send(psend.at[h, to], precv.at[h, v], pp_s.at[h, k], pp_r.at[h, k], at_v(k), hd)
    precv[:, v] = psend[:, v]

    for i in range(2):
        arrived(fresh.at[i, 1, zh], fx_s.at[i, 0], fx_r.at[i, 0])
        arrived(fresh.at[i, 0, 1 - zh], fx_s.at[i, 1], fx_r.at[i, 1])
    mine = flat_rows(qall[v])
    lane64 = lax.broadcasted_iota(jnp.int32, (1, ROWS), 1)
    f_tops, f_totals, f_accs = [], [], []
    fk = [flat_rows(fresh[0, b]) for b in range(2)]
    fv = [flat_rows(fresh[1, b]) for b in range(2)]
    for h in range(NH):
        parts = []
        for b in range(2):
            qb = mine[b * 32:(b + 1) * 32, head(h)]
            s = lax.dot_general(qb, fk[b][:, head(h)], (((1,), (1,)), ((), ())), preferred_element_type=F32) * SCALE
            parts.append(s + jnp.where(lane64 < counts[p if b == 0 else p_w], 0.0, NEG))
        s = jnp.concatenate(parts, axis=0)
        top = jnp.max(s, axis=1, keepdims=True)
        e = jnp.exp2(s - top)
        f_tops.append(top)
        f_totals.append(jnp.sum(e, axis=1, keepdims=True))
        eb = e.astype(BF16)
        f_accs.append(jnp.concatenate(
            [jnp.dot(eb[b * 32:(b + 1) * 32], fv[b][:, head(h)], preferred_element_type=F32) for b in range(2)], axis=0))
    f_stats = stats_rows(f_tops, f_totals)

    for k in (1, 3, 2):
        src = back(v, k)
        arrived(srecv.at[src], ps_s.at[k], ps_r.at[k])
    tt = [srecv[j, 0:8, 0:ROWS] for j in range(4)] + [f_stats[0:8]]
    ll = [srecv[j, 8:16, 0:ROWS] for j in range(4)] + [f_stats[8:16]]
    top = tt[0]
    for t in tt[1:]:
        top = jnp.maximum(top, t)
    fade = [jnp.exp2(t - top) for t in tt]
    total = fade[0] * ll[0]
    for f, l in zip(fade[1:], ll[1:]):
        total += f * l
    valid = lax.broadcasted_iota(jnp.int32, (8, ROWS), 0) < NH
    inv = 1.0 / jnp.where(valid, total, 1.0)
    share = jnp.concatenate([f * inv for f in fade] + [jnp.zeros((HD - 40, ROWS), F32)], axis=0)
    share = jnp.transpose(share)
    heads = []
    for h in range(NH):
        for k in (1, 3, 2):
            arrived(precv.at[h, back(v, k)], pp_s.at[h, k], pp_r.at[h, k])
        a = f_accs[h] * share[:, 32 + h:33 + h]
        for j in range(4):
            a += precv[h, j].astype(F32) * share[:, j * 8 + h:j * 8 + h + 1]
        heads.append(a)
    attended = jnp.concatenate(heads, axis=1).astype(BF16)

    for c in locals_[9:]:
        c.wait()
    for n in range(NC):
        c = slice(n * CW, (n + 1) * CW)
        proj = jnp.dot(attended, wv[:, c], preferred_element_type=F32).reshape(2, 4, 8, CW).astype(BF16)
        ys[1, :, :, c] = proj[1]
        ys[0, :, :, c] = proj[0]
        for k in (2, 1, 3):
            to = lax.rem(y + k, 4)
            send(ys.at[1, to, :, c], yr.at[1, y, :, c], y_s.at[1, n, k], y_r.at[1, n, k], p, at_y(k))
    for n in range(NC):
        c = slice(n * CW, (n + 1) * CW)
        for k in (2, 1, 3):
            to = lax.rem(y + k, 4)
            send(ys.at[0, to, :, c], yr.at[0, y, :, c], y_s.at[0, n, k], y_r.at[0, n, k], p, at_y(k))

    def sum_y(half, n):
        c = slice(n * CW, (n + 1) * CW)
        a = ys[half, y, :, c].astype(F32)
        for k in (1, 3, 2):
            src = lax.rem(y + 4 - k, 4)
            arrived(yr.at[half, src, :, c], y_s.at[half, n, k], y_r.at[half, n, k])
            a += yr[half, src, :, c].astype(F32)
        return a

    for n in range(NC):
        c = slice(n * CW, (n + 1) * CW)
        zs[:, c] = sum_y(1, n).astype(BF16)
        send(zs.at[:, c], zr.at[:, c], z_s.at[n], z_r.at[n], p_w, other + y)

    slot = hd * 8 + lax.broadcasted_iota(jnp.int32, (8, 1), 0)
    live = slot < counts[p]
    halves = [sum_y(0, n) for n in range(NC)]
    for n in range(NC):
        c = slice(n * CW, (n + 1) * CW)
        arrived(zr.at[:, c], z_s.at[n], z_r.at[n])
        whole = halves[n] + zr[:, c].astype(F32) + bias[:, c]
        out[:, c] = jnp.where(live, gate[:, c] * whole, 0.0).astype(BF16)

    for c in sends:
        c.wait_send()


def on_device(queries, keys, values, stale_keys, stale_values, patch_counts, out_weight, out_bias, gate_scale):
    dma = pltpu.SemaphoreType.DMA
    vm = pltpu.VMEM
    hbm = pl.BlockSpec(memory_space=pltpu.HBM)
    vmem = pl.BlockSpec(memory_space=pltpu.VMEM)

    def pair(*shape):
        return [dma(shape), dma(shape)]

    return pl.pallas_call(
        kernel,
        out_shape=jax.ShapeDtypeStruct((8, D), BF16),
        in_specs=[hbm] * 9,
        out_specs=vmem,
        scratch_shapes=[
            pltpu.SMEM((64,), jnp.int32),
            vm((1, D), F32),
            vm((1, D), F32),
            vm((4, 2, 4, 8, W3), BF16),
            vm((4, 2, ROWS, W3), BF16),
            vm((4, 2, ROWS, W3), BF16),
            vm((NH, 4, 2, ROWS, HD), BF16),
            vm((NH, 4, 2, ROWS, HD), BF16),
            vm((2, 2, 2, 4, 8, W3), BF16),
            vm((W3, D), BF16),
            vm((2, QS, KEYS), F32),
            vm((NH, QS, HD), F32),
            vm((NH, QS, KEYS), BF16),
            vm((NH, 4, ROWS, HD), BF16),
            vm((NH, 4, ROWS, HD), BF16),
            vm((4, 16, HD), F32),
            vm((4, 16, HD), F32),
            vm((2, 4, 8, D), BF16),
            vm((2, 4, 8, D), BF16),
            vm((8, D), BF16),
            vm((8, D), BF16),
            vm((4, 8, W3), BF16),
            vm((2, 4, 8, W3), BF16),
            dma((12,)),
            *pair(2, 4),
            *pair(2, 2, 4),
            *pair(2, 4),
            *pair(2, 4),
            *pair(2, NH),
            *pair(2, 4),
            *pair(2, NH, 4),
            *pair(2, NH, 4),
            *pair(2, 2),
            *pair(NH, 4),
            *pair(4),
            *pair(2, NC, 4),
            *pair(NC),
        ],
        compiler_params=pltpu.CompilerParams(collective_id=0, has_side_effects=True, vmem_limit_bytes=60 * 2**20),
        cost_estimate=pl.CostEstimate(flops=600_000_000, bytes_accessed=3_000_000, transcendentals=800_000),
    )(patch_counts, queries, keys, values, stale_keys, stale_values, out_weight, out_bias.reshape(1, D), gate_scale.reshape(1, D))


def solution(mesh):
    in_specs = (
        P(("patch", "head"), None),
        P(("patch", "head"), None),
        P(("patch", "head"), None),
        P("patch", "head"),
        P("patch", "head"),
        P(),
        P("head", None),
        P(),
        P(),
    )
    return jax.shard_map(on_device, mesh=mesh, in_specs=in_specs, out_specs=P(("patch", "head"), None), check_vma=False)
```

```python
import math

import jax
import jax.numpy as jnp
from jax import lax
from jax.experimental import pallas as pl
from jax.experimental.pallas import tpu as pltpu
from jax.sharding import PartitionSpec as P

MESH = pl.DeviceIdType.MESH
F32, BF16 = jnp.float32, jnp.bfloat16
HD = 128
NH = 3
W3 = HD * NH
D = 3072
ROWS = 64
KEYS = 8 * ROWS
QS = 4 * ROWS
HALF = QS // 2
NC = 4
CW = D // NC
LOG2E = 1.4426950408889634
SCALE = LOG2E / math.sqrt(HD)
NEG = -1e30


def flat_rows(ref_value):
    v = ref_value.astype(F32)
    return v.reshape(-1, v.shape[-1]).astype(BF16)


def kernel(
    counts_in, q_in, k_in, v_in, sk_in, sv_in, w_in, bias_in, gate_in, out,
    counts, bias, gate, qall, k0, v0, k1, v1, fresh, wv, off, acc, ebuf, psend, precv, ssend, srecv, ys, yr, zs, zr, cross,
    loc, qa_s, qa_r, qb_s, qb_r, fa_s, fa_r, fb_s, fb_r, cr_s, cr_r, g_s, g_r, kx_s, kx_r, kz_s, kz_r, kc_s, kc_r,
    x1_s, x1_r, c1_s, c1_r, xv_s, xv_r, fx_s, fx_r, pp_s, pp_r, ps_s, ps_r, y_s, y_r, z_s, z_r,
):
    p, hd = lax.axis_index("patch"), lax.axis_index("head")
    x, w, v, core = p // 16, (p // 8) % 2, (p // 2) % 4, p % 2
    zh, y = hd // 4, hd % 4

    def at_v(k):
        return p - v * 2 + lax.rem(v + k, 4) * 2

    def at_x(k):
        return p - x * 16 + lax.rem(x + k, 4) * 16

    def back(i, k):
        return lax.rem(i + 4 - k, 4)

    p_w = p - w * 8 + (1 - w) * 8
    p_c = p - core + (1 - core)
    other = (1 - zh) * 4

    def at_y(k):
        return zh * 4 + lax.rem(y + k, 4)

    def cols(h):
        return pl.ds(pl.multiple_of(h * W3, HD), W3)

    sends = []

    def send(src, dst, ss, rs, dp, dh):
        c = pltpu.make_async_remote_copy(src_ref=src, dst_ref=dst, send_sem=ss, recv_sem=rs, device_id=(dp, dh), device_id_type=MESH)
        c.start()
        sends.append(c)

    def arrived(dst, ss, rs):
        pltpu.make_async_remote_copy(src_ref=dst, dst_ref=dst, send_sem=ss, recv_sem=rs, device_id=(p_w, hd), device_id_type=MESH).wait_recv()

    barrier = pltpu.get_barrier_semaphore()
    greet = [(p_w, hd), (p_w, other + y), (p_c, hd)]
    greet += [(at_x(k), hd) for k in range(1, 4)]
    greet += [(at_x(k) - core + (1 - core), hd) for k in range(1, 4)]
    greet += [(at_v(k), hd) for k in range(1, 4)]
    greet += [(p, at_y(k)) for k in range(1, 4)]
    for d in greet:
        pl.semaphore_signal(barrier, inc=1, device_id=d, device_id_type=MESH)

    def head(h):
        return slice(h * HD, (h + 1) * HD)

    locals_ = [
        pltpu.make_async_copy(counts_in, counts, loc.at[0]),
        pltpu.make_async_copy(q_in.at[:, cols(hd)], qall.at[v, 0, y], loc.at[1]),
        pltpu.make_async_copy(sk_in, k0.at[x, core], loc.at[2]),
        pltpu.make_async_copy(sv_in, v0.at[x, core], loc.at[3]),
        pltpu.make_async_copy(k_in.at[:, cols(hd)], fresh.at[0, 0, zh, y], loc.at[4]),
        pltpu.make_async_copy(v_in.at[:, cols(hd)], fresh.at[1, 0, zh, y], loc.at[5]),
        pltpu.make_async_copy(bias_in, bias, loc.at[6]),
        pltpu.make_async_copy(gate_in, gate, loc.at[7]),
        pltpu.make_async_copy(w_in, wv, loc.at[8]),
    ]

    pl.semaphore_wait(barrier, len(greet))

    stale = ((sk_in, k0, k1), (sv_in, v0, v1))
    for i, (src, unused, buf) in enumerate(stale):
        for h in range(NH):
            send(src.at[:, head(h)], buf.at[h, x, core], kz_s.at[i, h], kz_r.at[i, h], p_w, hd)
    there = pl.ds(pl.multiple_of(other * W3, HD), 4 * W3)
    send(q_in.at[:, there], cross.at[0], cr_s.at[0], cr_r.at[0], p_w, other + y)
    for k in (2, 1, 3):
        send(q_in.at[:, cols(at_y(k))], qall.at[v, 0, y], qa_s.at[k], qa_r.at[k], p, at_y(k))
    for i, (src, buf, unused) in enumerate(stale):
        for k in (2, 1, 3):
            send(src, buf.at[x, core], kx_s.at[i, k], kx_r.at[i, k], at_x(k), hd)
        send(src, buf.at[x, core], kc_s.at[i, 0], kc_r.at[i, 0], p_c, hd)
    for c in locals_:
        c.start()
    for i, src in enumerate((k_in, v_in)):
        send(src.at[:, there], cross.at[1 + i], cr_s.at[1 + i], cr_r.at[1 + i], p_w, other + y)
    for i, src in enumerate((k_in, v_in)):
        for k in (2, 1, 3):
            send(src.at[:, cols(at_y(k))], fresh.at[i, 0, zh, y], fa_s.at[i, k], fa_r.at[i, k], p, at_y(k))

    locals_[0].wait()
    lane = lax.broadcasted_iota(jnp.int32, (1, KEYS), 1)
    row = lax.broadcasted_iota(jnp.int32, (HALF, 1), 0)
    dead = []
    for s in range(2):
        limit = jnp.zeros((1, KEYS), jnp.int32)
        for i in range(8):
            pp = (i // 2) * 16 + (w if s == 0 else 1 - w) * 8 + v * 2 + i % 2
            limit = jnp.where(lane // ROWS == i, counts[pp], limit)
        dead.append(jnp.where(lane % ROWS < limit, 0.0, NEG))
        off[s] = jnp.where((row // 32 == v) & (lane // ROWS == x * 2 + core), NEG, dead[s])

    def from_w(i, h):
        here = stale[i][2].at[h, x, core]
        arrived(here, kz_s.at[i, h], kz_r.at[i, h])
        if i == 0:
            for k in (2, 1, 3):
                send(here, here, x1_s.at[h, k], x1_r.at[h, k], at_x(k), hd)
            send(here, here, c1_s.at[h, 0], c1_r.at[h, 0], p_c, hd)
        else:
            for k in (2, 1, 3):
                send(here, here, xv_s.at[h, k, 0], xv_r.at[h, k, 0], at_x(k), hd)
                send(here, here, xv_s.at[h, k, 1], xv_r.at[h, k, 1], at_x(k) - core + (1 - core), hd)
            send(here, here, xv_s.at[h, 0, 1], xv_r.at[h, 0, 1], p_c, hd)

    def to_core(h):
        for k in (1, 3, 2):
            here = k1.at[h, back(x, k), core]
            arrived(here, x1_s.at[h, k], x1_r.at[h, k])
            send(here, here, c1_s.at[h, k], c1_r.at[h, k], p_c, hd)

    locals_[1].wait()
    for k in (1, 3, 2):
        arrived(qall.at[v, 0, back(y, k)], qa_s.at[k], qa_r.at[k])
    for k in (2, 1, 3):
        send(qall.at[v, 0], qall.at[v, 0], g_s.at[0, k], g_r.at[0, k], at_v(k), hd)

    from_w(0, 0)
    arrived(cross.at[0], cr_s.at[0], cr_r.at[0])

    def mine_of(i):
        return cross.at[i, :, pl.ds(pl.multiple_of(y * W3, HD), W3)]

    def to_of(i, k):
        return cross.at[i, :, pl.ds(pl.multiple_of(lax.rem(y + k, 4) * W3, HD), W3)]

    for k in (2, 1, 3):
        send(to_of(0, k), qall.at[v, 1, y], qb_s.at[k], qb_r.at[k], p, at_y(k))
    keep_q = pltpu.make_async_copy(mine_of(0), qall.at[v, 1, y], loc.at[9])
    keep_q.start()
    from_w(0, 1)
    for i in range(2):
        buf = stale[i][1]
        for k in (1, 3, 2):
            here = buf.at[back(x, k), core]
            arrived(here, kx_s.at[i, k], kx_r.at[i, k])
            send(here, here, kc_s.at[i, k], kc_r.at[i, k], p_c, hd)
    from_w(0, 2)
    from_w(1, 0)
    to_core(0)
    keep_q.wait()
    for k in (1, 3, 2):
        arrived(qall.at[v, 1, back(y, k)], qb_s.at[k], qb_r.at[k])
    for k in (2, 1, 3):
        send(qall.at[v, 1], qall.at[v, 1], g_s.at[1, k], g_r.at[1, k], at_v(k), hd)
    keep = []
    for i in range(2):
        arrived(cross.at[1 + i], cr_s.at[1 + i], cr_r.at[1 + i])
        for k in (2, 1, 3):
            send(to_of(1 + i, k), fresh.at[i, 1, 1 - zh, y], fb_s.at[i, k], fb_r.at[i, k], p, at_y(k))
        keep.append(pltpu.make_async_copy(mine_of(1 + i), fresh.at[i, 1, 1 - zh, y], loc.at[10 + i]))
        keep[i].start()
    from_w(1, 1)
    to_core(1)
    from_w(1, 2)
    for i in range(2):
        locals_[4 + i].wait()
        for k in (1, 3, 2):
            arrived(fresh.at[i, 0, zh, back(y, k)], fa_s.at[i, k], fa_r.at[i, k])
        send(fresh.at[i, 0, zh], fresh.at[i, 1, zh], fx_s.at[i, 0], fx_r.at[i, 0], p_w, hd)
    to_core(2)

    lanes = lax.broadcasted_iota(jnp.int32, (ROWS, HD), 1)

    def stats_rows(tops, totals):
        t = jnp.zeros((ROWS, HD), F32)
        for h in range(NH):
            t = jnp.where(lanes == h, tops[h], t)
            t = jnp.where(lanes == 8 + h, totals[h], t)
        return jnp.transpose(t)[:16, :]

    tops, totals = [[], []], [[], []]

    def shared(half):
        for k in (1, 3, 2):
            arrived(qall.at[back(v, k), half], g_s.at[half, k], g_r.at[half, k])
        return flat_rows(qall[:, half])

    def weigh(q, h, keys, mask):
        qk = lax.dot_general(q[:, head(h)], keys, (((1,), (1,)), ((), ())), preferred_element_type=F32)
        return qk * SCALE + mask

    def first(half, q):
        for h in range(NH):
            s = weigh(q, h, k0[:, :, :, head(h)].reshape(KEYS, HD), off[0] if half == 0 else dead[0])
            top = jnp.max(s, axis=1, keepdims=True)
            e = jnp.exp2(s - top)
            tops[half].append(top)
            totals[half].append(jnp.sum(e, axis=1, keepdims=True))
            acc[half, h] = jnp.dot(e.astype(BF16), v0[:, :, :, head(h)].reshape(KEYS, HD), preferred_element_type=F32)

    def second(half, q):
        for h in range(NH):
            s = weigh(q, h, k1[h].reshape(KEYS, HD), off[1] if half == 1 else dead[1])
            top = jnp.maximum(tops[half][h], jnp.max(s, axis=1, keepdims=True))
            fade = jnp.exp2(tops[half][h] - top)
            e = jnp.exp2(s - top)
            tops[half][h] = top
            totals[half][h] = totals[half][h] * fade + jnp.sum(e, axis=1, keepdims=True)
            ebuf[h, half * HALF:(half + 1) * HALF] = e.astype(BF16)
            acc[half, h] = acc[half, h] * fade

    q_a = shared(0)
    for i in range(2):
        locals_[2 + i].wait()
        for k in range(4):
            arrived(stale[i][1].at[back(x, k), 1 - core], kc_s.at[i, k], kc_r.at[i, k])
    first(0, q_a)
    for i in range(2):
        keep[i].wait()
        for k in (1, 3, 2):
            arrived(fresh.at[i, 1, 1 - zh, back(y, k)], fb_s.at[i, k], fb_r.at[i, k])
        send(fresh.at[i, 1, 1 - zh], fresh.at[i, 0, 1 - zh], fx_s.at[i, 1], fx_r.at[i, 1], p_w, hd)
    for h in range(NH):
        for k in range(4):
            arrived(k1.at[h, back(x, k), 1 - core], c1_s.at[h, k], c1_r.at[h, k])
    second(0, q_a)
    q_b = shared(1)
    first(1, q_b)
    second(1, q_b)

    for j in range(4):
        r = slice(j * 32, (j + 1) * 32)
        ssend[j, :, 0:ROWS] = stats_rows(*[[jnp.concatenate([t[0][h][r], t[1][h][r]], axis=0) for h in range(NH)] for t in (tops, totals)])
    for k in (2, 1, 3):
        to = lax.rem(v + k, 4)
        send(ssend.at[to], srecv.at[v], ps_s.at[k], ps_r.at[k], at_v(k), hd)
    srecv[v] = ssend[v]

    for h in range(NH):
        arrived(v1.at[h, x, 1 - core], xv_s.at[h, 0, 1], xv_r.at[h, 0, 1])
        for k in (1, 3, 2):
            arrived(v1.at[h, back(x, k), core], xv_s.at[h, k, 0], xv_r.at[h, k, 0])
            arrived(v1.at[h, back(x, k), 1 - core], xv_s.at[h, k, 1], xv_r.at[h, k, 1])
        a = jnp.dot(ebuf[h], v1[h].reshape(KEYS, HD), preferred_element_type=F32)
        for half in range(2):
            both = acc[half, h] + a[half * HALF:(half + 1) * HALF]
            psend[h, :, half] = both.astype(BF16).reshape(4, 32, HD)
        for k in (2, 1, 3):
            to = lax.rem(v + k, 4)
            send(psend.at[h, to], precv.at[h, v], pp_s.at[h, k], pp_r.at[h, k], at_v(k), hd)
    precv[:, v] = psend[:, v]

    for i in range(2):
        arrived(fresh.at[i, 1, zh], fx_s.at[i, 0], fx_r.at[i, 0])
        arrived(fresh.at[i, 0, 1 - zh], fx_s.at[i, 1], fx_r.at[i, 1])
    mine = flat_rows(qall[v])
    lane64 = lax.broadcasted_iota(jnp.int32, (1, ROWS), 1)
    f_tops, f_totals, f_accs = [], [], []
    fk = [flat_rows(fresh[0, b]) for b in range(2)]
    fv = [flat_rows(fresh[1, b]) for b in range(2)]
    for h in range(NH):
        parts = []
        for b in range(2):
            qb = mine[b * 32:(b + 1) * 32, head(h)]
            s = lax.dot_general(qb, fk[b][:, head(h)], (((1,), (1,)), ((), ())), preferred_element_type=F32) * SCALE
            parts.append(s + jnp.where(lane64 < counts[p if b == 0 else p_w], 0.0, NEG))
        s = jnp.concatenate(parts, axis=0)
        top = jnp.max(s, axis=1, keepdims=True)
        e = jnp.exp2(s - top)
        f_tops.append(top)
        f_totals.append(jnp.sum(e, axis=1, keepdims=True))
        eb = e.astype(BF16)
        f_accs.append(jnp.concatenate(
            [jnp.dot(eb[b * 32:(b + 1) * 32], fv[b][:, head(h)], preferred_element_type=F32) for b in range(2)], axis=0))
    f_stats = stats_rows(f_tops, f_totals)

    for k in (1, 3, 2):
        src = back(v, k)
        arrived(srecv.at[src], ps_s.at[k], ps_r.at[k])
    tt = [srecv[j, 0:8, 0:ROWS] for j in range(4)] + [f_stats[0:8]]
    ll = [srecv[j, 8:16, 0:ROWS] for j in range(4)] + [f_stats[8:16]]
    top = tt[0]
    for t in tt[1:]:
        top = jnp.maximum(top, t)
    fade = [jnp.exp2(t - top) for t in tt]
    total = fade[0] * ll[0]
    for f, l in zip(fade[1:], ll[1:]):
        total += f * l
    valid = lax.broadcasted_iota(jnp.int32, (8, ROWS), 0) < NH
    inv = 1.0 / jnp.where(valid, total, 1.0)
    share = jnp.concatenate([f * inv for f in fade] + [jnp.zeros((HD - 40, ROWS), F32)], axis=0)
    share = jnp.transpose(share)
    heads = []
    for h in range(NH):
        for k in (1, 3, 2):
            arrived(precv.at[h, back(v, k)], pp_s.at[h, k], pp_r.at[h, k])
        a = f_accs[h] * share[:, 32 + h:33 + h]
        for j in range(4):
            a += precv[h, j].reshape(ROWS, HD).astype(F32) * share[:, j * 8 + h:j * 8 + h + 1]
        heads.append(a)
    attended = jnp.concatenate(heads, axis=1).astype(BF16)

    for c in locals_[6:]:
        c.wait()
    for n in range(NC):
        c = slice(n * CW, (n + 1) * CW)
        proj = jnp.dot(attended, wv[:, c], preferred_element_type=F32).reshape(2, 4, 8, CW).astype(BF16)
        ys[1, :, :, c] = proj[1]
        ys[0, :, :, c] = proj[0]
        for k in (2, 1, 3):
            to = lax.rem(y + k, 4)
            send(ys.at[1, to, :, c], yr.at[1, y, :, c], y_s.at[1, n, k], y_r.at[1, n, k], p, at_y(k))
    for n in range(NC):
        c = slice(n * CW, (n + 1) * CW)
        for k in (2, 1, 3):
            to = lax.rem(y + k, 4)
            send(ys.at[0, to, :, c], yr.at[0, y, :, c], y_s.at[0, n, k], y_r.at[0, n, k], p, at_y(k))

    def sum_y(half, n):
        c = slice(n * CW, (n + 1) * CW)
        a = ys[half, y, :, c].astype(F32)
        for k in (1, 3, 2):
            src = lax.rem(y + 4 - k, 4)
            arrived(yr.at[half, src, :, c], y_s.at[half, n, k], y_r.at[half, n, k])
            a += yr[half, src, :, c].astype(F32)
        return a

    for n in range(NC):
        c = slice(n * CW, (n + 1) * CW)
        zs[:, c] = sum_y(1, n).astype(BF16)
        send(zs.at[:, c], zr.at[:, c], z_s.at[n], z_r.at[n], p_w, other + y)

    slot = hd * 8 + lax.broadcasted_iota(jnp.int32, (8, 1), 0)
    live = slot < counts[p]
    halves = [sum_y(0, n) for n in range(NC)]
    for n in range(NC):
        c = slice(n * CW, (n + 1) * CW)
        arrived(zr.at[:, c], z_s.at[n], z_r.at[n])
        whole = halves[n] + zr[:, c].astype(F32) + bias[:, c]
        out[:, c] = jnp.where(live, gate[:, c] * whole, 0.0).astype(BF16)

    for c in sends:
        c.wait_send()


def on_device(queries, keys, values, stale_keys, stale_values, patch_counts, out_weight, out_bias, gate_scale):
    dma = pltpu.SemaphoreType.DMA
    vm = pltpu.VMEM
    hbm = pl.BlockSpec(memory_space=pltpu.HBM)
    vmem = pl.BlockSpec(memory_space=pltpu.VMEM)

    def pair(*shape):
        return [dma(shape), dma(shape)]

    return pl.pallas_call(
        kernel,
        out_shape=jax.ShapeDtypeStruct((8, D), BF16),
        in_specs=[hbm] * 9,
        out_specs=vmem,
        scratch_shapes=[
            pltpu.SMEM((64,), jnp.int32),
            vm((1, D), F32),
            vm((1, D), F32),
            vm((4, 2, 4, 8, W3), BF16),
            vm((4, 2, ROWS, W3), BF16),
            vm((4, 2, ROWS, W3), BF16),
            vm((NH, 4, 2, ROWS, HD), BF16),
            vm((NH, 4, 2, ROWS, HD), BF16),
            vm((2, 2, 2, 4, 8, W3), BF16),
            vm((W3, D), BF16),
            vm((2, HALF, KEYS), F32),
            vm((2, NH, HALF, HD), F32),
            vm((NH, QS, KEYS), BF16),
            vm((NH, 4, 2, 32, HD), BF16),
            vm((NH, 4, 2, 32, HD), BF16),
            vm((4, 16, HD), F32),
            vm((4, 16, HD), F32),
            vm((2, 4, 8, D), BF16),
            vm((2, 4, 8, D), BF16),
            vm((8, D), BF16),
            vm((8, D), BF16),
            vm((3, 8, 4 * W3), BF16),
            dma((12,)),
            *pair(4),
            *pair(4),
            *pair(2, 4),
            *pair(2, 4),
            *pair(3),
            *pair(2, 4),
            *pair(2, 4),
            *pair(2, NH),
            *pair(2, 4),
            *pair(NH, 4),
            *pair(NH, 4),
            *pair(NH, 4, 2),
            *pair(2, 2),
            *pair(NH, 4),
            *pair(4),
            *pair(2, NC, 4),
            *pair(NC),
        ],
        compiler_params=pltpu.CompilerParams(collective_id=0, has_side_effects=True, vmem_limit_bytes=60 * 2**20),
        cost_estimate=pl.CostEstimate(flops=600_000_000, bytes_accessed=3_000_000, transcendentals=800_000),
    )(patch_counts, queries, keys, values, stale_keys, stale_values, out_weight, out_bias.reshape(1, D), gate_scale.reshape(1, D))


def solution(mesh):
    in_specs = (
        P(("patch", "head"), None),
        P(("patch", "head"), None),
        P(("patch", "head"), None),
        P("patch", "head"),
        P("patch", "head"),
        P(),
        P("head", None),
        P(),
        P(),
    )
    return jax.shard_map(on_device, mesh=mesh, in_specs=in_specs, out_specs=P(("patch", "head"), None), check_vma=False)
```

```python
import math

import jax
import jax.numpy as jnp
from jax import lax
from jax.experimental import pallas as pl
from jax.experimental.pallas import tpu as pltpu
from jax.sharding import PartitionSpec as P

MESH = pl.DeviceIdType.MESH
F32, BF16 = jnp.float32, jnp.bfloat16
HD = 128
NH = 3
W3 = HD * NH
D = 3072
ROWS = 64
KEYS = 8 * ROWS
QS = 4 * ROWS
NC = 4
CW = D // NC
LOG2E = 1.4426950408889634
SCALE = LOG2E / math.sqrt(HD)
NEG = -1e30


def flat_rows(ref_value):
    v = ref_value.astype(F32)
    return v.reshape(-1, v.shape[-1]).astype(BF16)


def kernel(
    counts_in, q_in, k_in, v_in, sk_in, sv_in, w_in, bias_in, gate_in, out,
    counts, bias, gate, qall, kb, v0, v1, fresh, wv, off, acc, ebuf, psend, precv, ssend, srecv, ys, yr, zs, zr,
    loc, s1q_s, s1q_r, s1f_s, s1f_r, g_s, g_r, kx_s, kx_r, kz_s, kz_r, kc_s, kc_r, xv_s, xv_r, fx_s, fx_r, pp_s, pp_r, ps_s, ps_r,
    y_s, y_r, z_s, z_r,
):
    p, hd = lax.axis_index("patch"), lax.axis_index("head")
    x, w, v, core = p // 16, (p // 8) % 2, (p // 2) % 4, p % 2
    zh, y = hd // 4, hd % 4

    def at_v(k):
        return p - v * 2 + lax.rem(v + k, 4) * 2

    def at_x(k):
        return p - x * 16 + lax.rem(x + k, 4) * 16

    def back(i, k):
        return lax.rem(i + 4 - k, 4)

    p_w = p - w * 8 + (1 - w) * 8
    p_c = p - core + (1 - core)
    other = (1 - zh) * 4

    def at_y(k):
        return zh * 4 + lax.rem(y + k, 4)

    def over_y(k):
        return other + lax.rem(y + k, 4)

    def cols(h):
        return pl.ds(pl.multiple_of(h * W3, HD), W3)

    sends = []

    def send(src, dst, ss, rs, dp, dh):
        c = pltpu.make_async_remote_copy(src_ref=src, dst_ref=dst, send_sem=ss, recv_sem=rs, device_id=(dp, dh), device_id_type=MESH)
        c.start()
        sends.append(c)

    def arrived(dst, ss, rs):
        pltpu.make_async_remote_copy(src_ref=dst, dst_ref=dst, send_sem=ss, recv_sem=rs, device_id=(p_w, hd), device_id_type=MESH).wait_recv()

    barrier = pltpu.get_barrier_semaphore()
    greet = [(p_w, hd), (p_c, hd)]
    greet += [(p_w, over_y(k)) for k in range(4)]
    greet += [(p, at_y(k)) for k in range(1, 4)]
    greet += [(at_v(k), hd) for k in range(1, 4)]
    greet += [(at_x(k), hd) for k in range(1, 4)]
    greet += [(at_x(k) - core + (1 - core), hd) for k in range(1, 4)]
    for d in greet:
        pl.semaphore_signal(barrier, inc=1, device_id=d, device_id_type=MESH)

    locals_ = [
        pltpu.make_async_copy(counts_in, counts, loc.at[0]),
        pltpu.make_async_copy(q_in.at[:, cols(hd)], qall.at[v, 0, y], loc.at[1]),
        pltpu.make_async_copy(sk_in, kb.at[0, x, core], loc.at[2]),
        pltpu.make_async_copy(sv_in, v0.at[x, core], loc.at[3]),
        pltpu.make_async_copy(k_in.at[:, cols(hd)], fresh.at[0, 0, zh, y], loc.at[4]),
        pltpu.make_async_copy(v_in.at[:, cols(hd)], fresh.at[1, 0, zh, y], loc.at[5]),
        pltpu.make_async_copy(bias_in, bias, loc.at[6]),
        pltpu.make_async_copy(gate_in, gate, loc.at[7]),
        pltpu.make_async_copy(w_in, wv, loc.at[8]),
    ]
    pl.semaphore_wait(barrier, len(greet))

    send(sk_in, kb.at[1, x, core], kz_s.at[NH], kz_r.at[NH], p_w, hd)
    for h in range(NH):
        send(sv_in.at[:, h * HD:(h + 1) * HD], v1.at[h, x, core], kz_s.at[h], kz_r.at[h], p_w, hd)
    for k in range(4):
        h = over_y(k)
        send(q_in.at[:, cols(h)], qall.at[v, 1, y], s1q_s.at[1, k], s1q_r.at[1, k], p_w, h)
    for k in range(1, 4):
        h = at_y(k)
        send(q_in.at[:, cols(h)], qall.at[v, 0, y], s1q_s.at[0, k], s1q_r.at[0, k], p, h)
    plane = ((sk_in, kb.at[0]), (sv_in, v0))
    for i, (src, buf) in enumerate(plane):
        for k in (2, 1, 3):
            send(src, buf.at[x, core], kx_s.at[i, k], kx_r.at[i, k], at_x(k), hd)
        send(src, buf.at[x, core], kc_s.at[i, 0], kc_r.at[i, 0], p_c, hd)
    for c in locals_:
        c.start()
    for i, src in enumerate((k_in, v_in)):
        for k in range(4):
            h = over_y(k)
            send(src.at[:, cols(h)], fresh.at[i, 1, zh, y], s1f_s.at[i, 1, k], s1f_r.at[i, 1, k], p_w, h)
        for k in range(1, 4):
            h = at_y(k)
            send(src.at[:, cols(h)], fresh.at[i, 0, zh, y], s1f_s.at[i, 0, k], s1f_r.at[i, 0, k], p, h)

    locals_[0].wait()
    lane = lax.broadcasted_iota(jnp.int32, (1, KEYS), 1)
    row = lax.broadcasted_iota(jnp.int32, (QS, 1), 0)
    for s in range(2):
        limit = jnp.zeros((1, KEYS), jnp.int32)
        for i in range(8):
            pp = (i // 2) * 16 + (w if s == 0 else 1 - w) * 8 + v * 2 + i % 2
            limit = jnp.where(lane // ROWS == i, counts[pp], limit)
        dead = jnp.where(lane % ROWS < limit, 0.0, NEG)
        own_rows = (row // 32) == v * 2 + s
        own_keys = (lane // ROWS) == x * 2 + core
        off[s] = jnp.where(own_rows & own_keys, NEG, dead)

    locals_[1].wait()
    for k in range(1, 4):
        arrived(qall.at[v, 0, back(y, k)], s1q_s.at[0, k], s1q_r.at[0, k])
    for k in (2, 1, 3):
        send(qall.at[v, 0], qall.at[v, 0], g_s.at[0, k], g_r.at[0, k], at_v(k), hd)
    for k in range(4):
        arrived(qall.at[v, 1, back(y, k)], s1q_s.at[1, k], s1q_r.at[1, k])
    for k in (2, 1, 3):
        send(qall.at[v, 1], qall.at[v, 1], g_s.at[1, k], g_r.at[1, k], at_v(k), hd)

    for i in range(2):
        for k in (1, 3, 2):
            here = plane[i][1].at[back(x, k), core]
            arrived(here, kx_s.at[i, k], kx_r.at[i, k])
            send(here, here, kc_s.at[i, k], kc_r.at[i, k], p_c, hd)
    here = kb.at[1, x, core]
    arrived(here, kz_s.at[NH], kz_r.at[NH])
    for k in (2, 1, 3):
        send(here, here, kx_s.at[2, k], kx_r.at[2, k], at_x(k), hd)
    send(here, here, kc_s.at[2, 0], kc_r.at[2, 0], p_c, hd)
    for h in range(NH):
        here = v1.at[h, x, core]
        arrived(here, kz_s.at[h], kz_r.at[h])
        for k in (2, 1, 3):
            send(here, here, xv_s.at[h, k, 0], xv_r.at[h, k, 0], at_x(k), hd)
            send(here, here, xv_s.at[h, k, 1], xv_r.at[h, k, 1], at_x(k) - core + (1 - core), hd)
        send(here, here, xv_s.at[h, 0, 1], xv_r.at[h, 0, 1], p_c, hd)

    locals_[4].wait()
    locals_[5].wait()
    for i in range(2):
        for k in range(1, 4):
            arrived(fresh.at[i, 0, zh, back(y, k)], s1f_s.at[i, 0, k], s1f_r.at[i, 0, k])
        send(fresh.at[i, 0, zh], fresh.at[i, 1, zh], fx_s.at[i, 0], fx_r.at[i, 0], p_w, hd)
        for k in range(4):
            arrived(fresh.at[i, 1, 1 - zh, back(y, k)], s1f_s.at[i, 1, k], s1f_r.at[i, 1, k])
        send(fresh.at[i, 1, 1 - zh], fresh.at[i, 0, 1 - zh], fx_s.at[i, 1], fx_r.at[i, 1], p_w, hd)

    lanes = lax.broadcasted_iota(jnp.int32, (ROWS, HD), 1)

    def stats_rows(tops, totals):
        t = jnp.zeros((ROWS, HD), F32)
        for h in range(NH):
            t = jnp.where(lanes == h, tops[h], t)
            t = jnp.where(lanes == 8 + h, totals[h], t)
        return jnp.transpose(t)[:16, :]

    def head(h):
        return slice(h * HD, (h + 1) * HD)

    def scores(s, h):
        kh = kb[s, :, :, :, head(h)].reshape(KEYS, HD)
        qk = lax.dot_general(queries[:, head(h)], kh, (((1,), (1,)), ((), ())), preferred_element_type=F32)
        return qk * SCALE + off[s]

    for half in range(2):
        for k in range(1, 4):
            arrived(qall.at[back(v, k), half], g_s.at[half, k], g_r.at[half, k])
    queries = flat_rows(qall[...])
    locals_[2].wait()
    locals_[3].wait()
    for i in range(2):
        for k in range(4):
            arrived(plane[i][1].at[back(x, k), 1 - core], kc_s.at[i, k], kc_r.at[i, k])
    tops, totals = [], []
    for h in range(NH):
        s = scores(0, h)
        top = jnp.max(s, axis=1, keepdims=True)
        e = jnp.exp2(s - top)
        tops.append(top)
        totals.append(jnp.sum(e, axis=1, keepdims=True))
        acc[h] = jnp.dot(e.astype(BF16), v0[:, :, :, head(h)].reshape(KEYS, HD), preferred_element_type=F32)

    for k in (1, 3, 2):
        here = kb.at[1, back(x, k), core]
        arrived(here, kx_s.at[2, k], kx_r.at[2, k])
        send(here, here, kc_s.at[2, k], kc_r.at[2, k], p_c, hd)
    for k in range(4):
        arrived(kb.at[1, back(x, k), 1 - core], kc_s.at[2, k], kc_r.at[2, k])
    for h in range(NH):
        s = scores(1, h)
        top = jnp.maximum(tops[h], jnp.max(s, axis=1, keepdims=True))
        fade = jnp.exp2(tops[h] - top)
        e = jnp.exp2(s - top)
        tops[h] = top
        totals[h] = totals[h] * fade + jnp.sum(e, axis=1, keepdims=True)
        ebuf[h] = e.astype(BF16)
        acc[h] = acc[h] * fade
    for j in range(4):
        r = slice(j * ROWS, (j + 1) * ROWS)
        ssend[j, :, 0:ROWS] = stats_rows([t[r] for t in tops], [t[r] for t in totals])
    for k in (2, 1, 3):
        to = lax.rem(v + k, 4)
        send(ssend.at[to], srecv.at[v], ps_s.at[k], ps_r.at[k], at_v(k), hd)
    srecv[v] = ssend[v]
    for h in range(NH):
        arrived(v1.at[h, x, 1 - core], xv_s.at[h, 0, 1], xv_r.at[h, 0, 1])
        for k in (1, 3, 2):
            arrived(v1.at[h, back(x, k), core], xv_s.at[h, k, 0], xv_r.at[h, k, 0])
            arrived(v1.at[h, back(x, k), 1 - core], xv_s.at[h, k, 1], xv_r.at[h, k, 1])
        a = acc[h] + jnp.dot(ebuf[h], v1[h].reshape(KEYS, HD), preferred_element_type=F32)
        a = a.reshape(4, 2, 32, HD).astype(BF16)
        for half in (1, 0):
            psend[h, half] = a[:, half]
            for k in (2, 1, 3):
                to = lax.rem(v + k, 4)
                send(psend.at[h, half, to], precv.at[h, half, v], pp_s.at[h, half, k], pp_r.at[h, half, k], at_v(k), hd)
    precv[:, :, v] = psend[:, :, v]

    arrived(fresh.at[0, 1, zh], fx_s.at[0, 0], fx_r.at[0, 0])
    arrived(fresh.at[0, 0, 1 - zh], fx_s.at[0, 1], fx_r.at[0, 1])
    mine = flat_rows(qall[v])
    lane64 = lax.broadcasted_iota(jnp.int32, (1, ROWS), 1)
    f_tops, f_totals, f_exp = [], [], []
    fk = [flat_rows(fresh[0, b]) for b in range(2)]
    for h in range(NH):
        parts = []
        for b in range(2):
            qb = mine[b * 32:(b + 1) * 32, head(h)]
            s = lax.dot_general(qb, fk[b][:, head(h)], (((1,), (1,)), ((), ())), preferred_element_type=F32) * SCALE
            parts.append(s + jnp.where(lane64 < counts[p if b == 0 else p_w], 0.0, NEG))
        s = jnp.concatenate(parts, axis=0)
        top = jnp.max(s, axis=1, keepdims=True)
        e = jnp.exp2(s - top)
        f_tops.append(top)
        f_totals.append(jnp.sum(e, axis=1, keepdims=True))
        f_exp.append(e.astype(BF16))
    f_stats = stats_rows(f_tops, f_totals)

    for k in (1, 3, 2):
        src = back(v, k)
        arrived(srecv.at[src], ps_s.at[k], ps_r.at[k])
    tt = [srecv[j, 0:8, 0:ROWS] for j in range(4)] + [f_stats[0:8]]
    ll = [srecv[j, 8:16, 0:ROWS] for j in range(4)] + [f_stats[8:16]]
    top = tt[0]
    for t in tt[1:]:
        top = jnp.maximum(top, t)
    fade = [jnp.exp2(t - top) for t in tt]
    total = fade[0] * ll[0]
    for f, l in zip(fade[1:], ll[1:]):
        total += f * l
    valid = lax.broadcasted_iota(jnp.int32, (8, ROWS), 0) < NH
    inv = 1.0 / jnp.where(valid, total, 1.0)
    share = jnp.concatenate([f * inv for f in fade] + [jnp.zeros((HD - 40, ROWS), F32)], axis=0)
    share = jnp.transpose(share)
    arrived(fresh.at[1, 1, zh], fx_s.at[1, 0], fx_r.at[1, 0])
    arrived(fresh.at[1, 0, 1 - zh], fx_s.at[1, 1], fx_r.at[1, 1])
    fv = [flat_rows(fresh[1, b]) for b in range(2)]
    for c in locals_[6:]:
        c.wait()
    for half in (1, 0):
        r = slice(half * 32, (half + 1) * 32)
        heads = []
        for h in range(NH):
            for k in (1, 3, 2):
                arrived(precv.at[h, half, back(v, k)], pp_s.at[h, half, k], pp_r.at[h, half, k])
            a = jnp.dot(f_exp[h][r], fv[half][:, head(h)], preferred_element_type=F32) * share[r, 32 + h:33 + h]
            for j in range(4):
                a += precv[h, half, j].astype(F32) * share[r, j * 8 + h:j * 8 + h + 1]
            heads.append(a)
        attended = jnp.concatenate(heads, axis=1).astype(BF16)
        for n in range(NC):
            c = slice(n * CW, (n + 1) * CW)
            proj = jnp.dot(attended, wv[:, c], preferred_element_type=F32)
            ys[half, :, :, c] = proj.reshape(4, 8, CW).astype(BF16)
            for k in (2, 1, 3):
                to = lax.rem(y + k, 4)
                send(ys.at[half, to, :, c], yr.at[half, y, :, c], y_s.at[half, n, k], y_r.at[half, n, k], p, at_y(k))

    def sum_y(half, n):
        c = slice(n * CW, (n + 1) * CW)
        a = ys[half, y, :, c].astype(F32)
        for k in (1, 3, 2):
            src = lax.rem(y + 4 - k, 4)
            arrived(yr.at[half, src, :, c], y_s.at[half, n, k], y_r.at[half, n, k])
            a += yr[half, src, :, c].astype(F32)
        return a

    for n in range(NC):
        c = slice(n * CW, (n + 1) * CW)
        zs[:, c] = sum_y(1, n).astype(BF16)
        send(zs.at[:, c], zr.at[:, c], z_s.at[n], z_r.at[n], p_w, other + y)

    slot = hd * 8 + lax.broadcasted_iota(jnp.int32, (8, 1), 0)
    live = slot < counts[p]
    halves = [sum_y(0, n) for n in range(NC)]
    for n in range(NC):
        c = slice(n * CW, (n + 1) * CW)
        arrived(zr.at[:, c], z_s.at[n], z_r.at[n])
        whole = halves[n] + zr[:, c].astype(F32) + bias[:, c]
        out[:, c] = jnp.where(live, gate[:, c] * whole, 0.0).astype(BF16)

    for c in sends:
        c.wait_send()


def on_device(queries, keys, values, stale_keys, stale_values, patch_counts, out_weight, out_bias, gate_scale):
    dma = pltpu.SemaphoreType.DMA
    vm = pltpu.VMEM
    hbm = pl.BlockSpec(memory_space=pltpu.HBM)
    vmem = pl.BlockSpec(memory_space=pltpu.VMEM)

    def pair(*shape):
        return [dma(shape), dma(shape)]

    return pl.pallas_call(
        kernel,
        out_shape=pltpu.VMEM((8, D), BF16),
        in_specs=[hbm] * 9,
        out_specs=vmem,
        scratch_shapes=[
            pltpu.SMEM((64,), jnp.int32),
            vm((1, D), F32),
            vm((1, D), F32),
            vm((4, 2, 4, 8, W3), BF16),
            vm((2, 4, 2, ROWS, W3), BF16),
            vm((4, 2, ROWS, W3), BF16),
            vm((NH, 4, 2, ROWS, HD), BF16),
            vm((2, 2, 2, 4, 8, W3), BF16),
            vm((W3, D), BF16),
            vm((2, QS, KEYS), F32),
            vm((NH, QS, HD), F32),
            vm((NH, QS, KEYS), BF16),
            vm((NH, 2, 4, 32, HD), BF16),
            vm((NH, 2, 4, 32, HD), BF16),
            vm((4, 16, HD), F32),
            vm((4, 16, HD), F32),
            vm((2, 4, 8, D), BF16),
            vm((2, 4, 8, D), BF16),
            vm((8, D), BF16),
            vm((8, D), BF16),
            dma((9,)),
            *pair(2, 4),
            *pair(2, 2, 4),
            *pair(2, 4),
            *pair(3, 4),
            *pair(NH + 1),
            *pair(3, 4),
            *pair(NH, 4, 2),
            *pair(2, 2),
            *pair(NH, 2, 4),
            *pair(4),
            *pair(2, NC, 4),
            *pair(NC),
        ],
        compiler_params=pltpu.CompilerParams(collective_id=0, has_side_effects=True, vmem_limit_bytes=60 * 2**20),
        cost_estimate=pl.CostEstimate(flops=600_000_000, bytes_accessed=3_000_000, transcendentals=800_000),
    )(patch_counts, queries, keys, values, stale_keys, stale_values, out_weight, out_bias.reshape(1, D), gate_scale.reshape(1, D))


def solution(mesh):
    in_specs = (
        P(("patch", "head"), None),
        P(("patch", "head"), None),
        P(("patch", "head"), None),
        P("patch", "head"),
        P("patch", "head"),
        P(),
        P("head", None),
        P(),
        P(),
    )
    return jax.shard_map(on_device, mesh=mesh, in_specs=in_specs, out_specs=P(("patch", "head"), None), check_vma=False)
```

```python
import math

import jax
import jax.numpy as jnp
from jax import lax
from jax.experimental import pallas as pl
from jax.experimental.pallas import tpu as pltpu
from jax.sharding import PartitionSpec as P

MESH = pl.DeviceIdType.MESH
F32, BF16 = jnp.float32, jnp.bfloat16
HD = 128
NH = 3
W3 = HD * NH
D = 3072
ROWS = 64
KEYS = 8 * ROWS
QS = 4 * ROWS
NC = 4
CW = D // NC
LOG2E = 1.4426950408889634
SCALE = LOG2E / math.sqrt(HD)
NEG = -1e30


def flat_rows(ref_value):
    v = ref_value.astype(F32)
    return v.reshape(-1, v.shape[-1]).astype(BF16)


def kernel(
    counts_in, q_in, k_in, v_in, sk_in, sv_in, w_in, bias_in, gate_in, out,
    counts, bias, gate, qs, ks, vs, qall, kb, v0, v1, fresh, wv, off, acc, ebuf, psend, precv, ssend, srecv, ys, yr, zs, zr,
    loc, s1q_s, s1q_r, s1f_s, s1f_r, g_s, g_r, kx_s, kx_r, kz_s, kz_r, kc_s, kc_r, xv_s, xv_r, fx_s, fx_r, pp_s, pp_r, ps_s, ps_r,
    y_s, y_r, z_s, z_r,
):
    p, hd = lax.axis_index("patch"), lax.axis_index("head")
    x, w, v, core = p // 16, (p // 8) % 2, (p // 2) % 4, p % 2
    zh, y = hd // 4, hd % 4

    def at_v(k):
        return p - v * 2 + lax.rem(v + k, 4) * 2

    def at_x(k):
        return p - x * 16 + lax.rem(x + k, 4) * 16

    def back(i, k):
        return lax.rem(i + 4 - k, 4)

    p_w = p - w * 8 + (1 - w) * 8
    p_c = p - core + (1 - core)
    other = (1 - zh) * 4

    def at_y(k):
        return zh * 4 + lax.rem(y + k, 4)

    def over_y(k):
        return other + lax.rem(y + k, 4)

    def cols(h):
        return pl.ds(pl.multiple_of(h * W3, HD), W3)

    sends = []

    def send(src, dst, ss, rs, dp, dh):
        c = pltpu.make_async_remote_copy(src_ref=src, dst_ref=dst, send_sem=ss, recv_sem=rs, device_id=(dp, dh), device_id_type=MESH)
        c.start()
        sends.append(c)

    def arrived(dst, ss, rs):
        pltpu.make_async_remote_copy(src_ref=dst, dst_ref=dst, send_sem=ss, recv_sem=rs, device_id=(p_w, hd), device_id_type=MESH).wait_recv()

    barrier = pltpu.get_barrier_semaphore()
    greet = [(p_w, hd), (p_c, hd)]
    greet += [(p_w, over_y(k)) for k in range(4)]
    greet += [(p, at_y(k)) for k in range(1, 4)]
    greet += [(at_v(k), hd) for k in range(1, 4)]
    greet += [(at_x(k), hd) for k in range(1, 4)]
    greet += [(at_x(k) - core + (1 - core), hd) for k in range(1, 4)]
    for d in greet:
        pl.semaphore_signal(barrier, inc=1, device_id=d, device_id_type=MESH)

    locals_ = [
        pltpu.make_async_copy(counts_in, counts, loc.at[0]),
        pltpu.make_async_copy(q_in.at[:, cols(hd)], qall.at[v, 0, y], loc.at[1]),
        pltpu.make_async_copy(sk_in, kb.at[0, x, core], loc.at[2]),
        pltpu.make_async_copy(sv_in, v0.at[x, core], loc.at[3]),
        pltpu.make_async_copy(k_in.at[:, cols(hd)], fresh.at[0, 0, zh, y], loc.at[4]),
        pltpu.make_async_copy(v_in.at[:, cols(hd)], fresh.at[1, 0, zh, y], loc.at[5]),
        pltpu.make_async_copy(bias_in, bias, loc.at[6]),
        pltpu.make_async_copy(gate_in, gate, loc.at[7]),
        pltpu.make_async_copy(w_in, wv, loc.at[8]),
        pltpu.make_async_copy(q_in, qs, loc.at[9]),
        pltpu.make_async_copy(k_in, ks, loc.at[10]),
        pltpu.make_async_copy(v_in, vs, loc.at[11]),
    ]
    for i in (2, 3, 9, 10, 11, 1, 4, 5, 0, 6, 7, 8):
        locals_[i].start()

    pl.semaphore_wait(barrier, len(greet))

    locals_[2].wait()
    send(kb.at[0, x, core], kb.at[1, x, core], kz_s.at[NH], kz_r.at[NH], p_w, hd)
    locals_[3].wait()
    for h in range(NH):
        send(v0.at[x, core, :, h * HD:(h + 1) * HD], v1.at[h, x, core], kz_s.at[h], kz_r.at[h], p_w, hd)
    locals_[9].wait()
    for k in range(4):
        h = over_y(k)
        send(qs.at[:, cols(h)], qall.at[v, 1, y], s1q_s.at[1, k], s1q_r.at[1, k], p_w, h)
    for k in range(1, 4):
        h = at_y(k)
        send(qs.at[:, cols(h)], qall.at[v, 0, y], s1q_s.at[0, k], s1q_r.at[0, k], p, h)
    plane = ((kb.at[0, x, core], kb.at[0]), (v0.at[x, core], v0))
    for i, (src, buf) in enumerate(plane):
        for k in (2, 1, 3):
            send(src, buf.at[x, core], kx_s.at[i, k], kx_r.at[i, k], at_x(k), hd)
        send(src, buf.at[x, core], kc_s.at[i, 0], kc_r.at[i, 0], p_c, hd)
    locals_[10].wait()
    locals_[11].wait()
    for i, src in enumerate((ks, vs)):
        for k in range(4):
            h = over_y(k)
            send(src.at[:, cols(h)], fresh.at[i, 1, zh, y], s1f_s.at[i, 1, k], s1f_r.at[i, 1, k], p_w, h)
        for k in range(1, 4):
            h = at_y(k)
            send(src.at[:, cols(h)], fresh.at[i, 0, zh, y], s1f_s.at[i, 0, k], s1f_r.at[i, 0, k], p, h)

    locals_[0].wait()
    lane = lax.broadcasted_iota(jnp.int32, (1, KEYS), 1)
    row = lax.broadcasted_iota(jnp.int32, (QS, 1), 0)
    for s in range(2):
        limit = jnp.zeros((1, KEYS), jnp.int32)
        for i in range(8):
            pp = (i // 2) * 16 + (w if s == 0 else 1 - w) * 8 + v * 2 + i % 2
            limit = jnp.where(lane // ROWS == i, counts[pp], limit)
        dead = jnp.where(lane % ROWS < limit, 0.0, NEG)
        own_rows = (row // 32) == v * 2 + s
        own_keys = (lane // ROWS) == x * 2 + core
        off[s] = jnp.where(own_rows & own_keys, NEG, dead)

    locals_[1].wait()
    for k in range(1, 4):
        arrived(qall.at[v, 0, back(y, k)], s1q_s.at[0, k], s1q_r.at[0, k])
    for k in (2, 1, 3):
        send(qall.at[v, 0], qall.at[v, 0], g_s.at[0, k], g_r.at[0, k], at_v(k), hd)
    for k in range(4):
        arrived(qall.at[v, 1, back(y, k)], s1q_s.at[1, k], s1q_r.at[1, k])
    for k in (2, 1, 3):
        send(qall.at[v, 1], qall.at[v, 1], g_s.at[1, k], g_r.at[1, k], at_v(k), hd)

    for i in range(2):
        for k in (1, 3, 2):
            here = plane[i][1].at[back(x, k), core]
            arrived(here, kx_s.at[i, k], kx_r.at[i, k])
            send(here, here, kc_s.at[i, k], kc_r.at[i, k], p_c, hd)
    here = kb.at[1, x, core]
    arrived(here, kz_s.at[NH], kz_r.at[NH])
    for k in (2, 1, 3):
        send(here, here, kx_s.at[2, k], kx_r.at[2, k], at_x(k), hd)
    send(here, here, kc_s.at[2, 0], kc_r.at[2, 0], p_c, hd)
    locals_[4].wait()
    locals_[5].wait()
    for i in range(2):
        for k in range(1, 4):
            arrived(fresh.at[i, 0, zh, back(y, k)], s1f_s.at[i, 0, k], s1f_r.at[i, 0, k])
        send(fresh.at[i, 0, zh], fresh.at[i, 1, zh], fx_s.at[i, 0], fx_r.at[i, 0], p_w, hd)
    for h in range(NH):
        here = v1.at[h, x, core]
        arrived(here, kz_s.at[h], kz_r.at[h])
        for k in (2, 1, 3):
            send(here, here, xv_s.at[h, k, 0], xv_r.at[h, k, 0], at_x(k), hd)
            send(here, here, xv_s.at[h, k, 1], xv_r.at[h, k, 1], at_x(k) - core + (1 - core), hd)
        send(here, here, xv_s.at[h, 0, 1], xv_r.at[h, 0, 1], p_c, hd)

    for i in range(2):
        for k in range(4):
            arrived(fresh.at[i, 1, 1 - zh, back(y, k)], s1f_s.at[i, 1, k], s1f_r.at[i, 1, k])
        send(fresh.at[i, 1, 1 - zh], fresh.at[i, 0, 1 - zh], fx_s.at[i, 1], fx_r.at[i, 1], p_w, hd)

    def stats_rows(tops, totals):
        shape = (tops[0].shape[0], HD)
        lanes = lax.broadcasted_iota(jnp.int32, shape, 1)
        t = jnp.zeros(shape, F32)
        for h in range(NH):
            t = jnp.where(lanes == h, tops[h], t)
            t = jnp.where(lanes == 8 + h, totals[h], t)
        return jnp.transpose(t)[:16, :]

    def head(h):
        return slice(h * HD, (h + 1) * HD)

    def scores(s, h):
        kh = kb[s, :, :, :, head(h)].reshape(KEYS, HD)
        qk = lax.dot_general(queries[:, head(h)], kh, (((1,), (1,)), ((), ())), preferred_element_type=F32)
        return qk * SCALE + off[s]

    for half in range(2):
        for k in range(1, 4):
            arrived(qall.at[back(v, k), half], g_s.at[half, k], g_r.at[half, k])
    queries = flat_rows(qall[...])
    for i in range(2):
        for k in range(4):
            arrived(plane[i][1].at[back(x, k), 1 - core], kc_s.at[i, k], kc_r.at[i, k])
    tops, totals = [], []
    for h in range(NH):
        s = scores(0, h)
        top = jnp.max(s, axis=1, keepdims=True)
        e = jnp.exp2(s - top)
        tops.append(top)
        totals.append(jnp.sum(e, axis=1, keepdims=True))
        acc[h] = jnp.dot(e.astype(BF16), v0[:, :, :, head(h)].reshape(KEYS, HD), preferred_element_type=F32)

    for k in (1, 3, 2):
        here = kb.at[1, back(x, k), core]
        arrived(here, kx_s.at[2, k], kx_r.at[2, k])
        send(here, here, kc_s.at[2, k], kc_r.at[2, k], p_c, hd)
    for k in range(4):
        arrived(kb.at[1, back(x, k), 1 - core], kc_s.at[2, k], kc_r.at[2, k])
    for h in range(NH):
        s = scores(1, h)
        top = jnp.maximum(tops[h], jnp.max(s, axis=1, keepdims=True))
        fade = jnp.exp2(tops[h] - top)
        e = jnp.exp2(s - top)
        tops[h] = top
        totals[h] = totals[h] * fade + jnp.sum(e, axis=1, keepdims=True)
        ebuf[h] = e.astype(BF16)
        acc[h] = acc[h] * fade
    for j in range(4):
        r = slice(j * ROWS, (j + 1) * ROWS)
        ssend[j, :, 0:ROWS] = stats_rows([t[r] for t in tops], [t[r] for t in totals])
    for k in (2, 1, 3):
        to = lax.rem(v + k, 4)
        send(ssend.at[to], srecv.at[v], ps_s.at[k], ps_r.at[k], at_v(k), hd)
    srecv[v] = ssend[v]
    for h in range(NH):
        arrived(v1.at[h, x, 1 - core], xv_s.at[h, 0, 1], xv_r.at[h, 0, 1])
        for k in (1, 3, 2):
            arrived(v1.at[h, back(x, k), core], xv_s.at[h, k, 0], xv_r.at[h, k, 0])
            arrived(v1.at[h, back(x, k), 1 - core], xv_s.at[h, k, 1], xv_r.at[h, k, 1])
        a = acc[h] + jnp.dot(ebuf[h], v1[h].reshape(KEYS, HD), preferred_element_type=F32)
        a = a.reshape(4, 2, 32, HD).astype(BF16)
        for half in (1, 0):
            psend[h, half] = a[:, half]
            for k in (2, 1, 3) if half == 1 else ():
                to = lax.rem(v + k, 4)
                send(psend.at[h, half, to], precv.at[h, half, v], pp_s.at[h, half, k], pp_r.at[h, half, k], at_v(k), hd)
    for h in range(NH):
        for k in (2, 1, 3):
            to = lax.rem(v + k, 4)
            send(psend.at[h, 0, to], precv.at[h, 0, v], pp_s.at[h, 0, k], pp_r.at[h, 0, k], at_v(k), hd)
    precv[:, :, v] = psend[:, :, v]

    lane64 = lax.broadcasted_iota(jnp.int32, (1, ROWS), 1)
    valid = lax.broadcasted_iota(jnp.int32, (8, 32), 0) < NH
    for half in (1, 0):
        r = slice(half * 32, (half + 1) * 32)
        mine = flat_rows(qall[v, half])
        new = zh if half == 1 else 1 - zh
        arrived(fresh.at[0, half, new], fx_s.at[0, 1 - half], fx_r.at[0, 1 - half])
        fk = flat_rows(fresh[0, half])
        mask = jnp.where(lane64 < counts[p if half == 0 else p_w], 0.0, NEG)
        f_tops, f_totals, f_exp = [], [], []
        for h in range(NH):
            s = lax.dot_general(mine[:, head(h)], fk[:, head(h)], (((1,), (1,)), ((), ())), preferred_element_type=F32)
            s = s * SCALE + mask
            top = jnp.max(s, axis=1, keepdims=True)
            e = jnp.exp2(s - top)
            f_tops.append(top)
            f_totals.append(jnp.sum(e, axis=1, keepdims=True))
            f_exp.append(e.astype(BF16))
        f_stats = stats_rows(f_tops, f_totals)
        if half == 1:
            for c in locals_[6:9]:
                c.wait()
            for k in (1, 3, 2):
                arrived(srecv.at[back(v, k)], ps_s.at[k], ps_r.at[k])
        tt = [srecv[j, 0:8, r] for j in range(4)] + [f_stats[0:8]]
        ll = [srecv[j, 8:16, r] for j in range(4)] + [f_stats[8:16]]
        top = tt[0]
        for t in tt[1:]:
            top = jnp.maximum(top, t)
        fade = [jnp.exp2(t - top) for t in tt]
        total = fade[0] * ll[0]
        for f, l in zip(fade[1:], ll[1:]):
            total += f * l
        inv = 1.0 / jnp.where(valid, total, 1.0)
        share = jnp.concatenate([f * inv for f in fade] + [jnp.zeros((HD - 40, 32), F32)], axis=0)
        share = jnp.transpose(share)
        arrived(fresh.at[1, half, new], fx_s.at[1, 1 - half], fx_r.at[1, 1 - half])
        fv = flat_rows(fresh[1, half])
        heads = [jnp.dot(f_exp[h], fv[:, head(h)], preferred_element_type=F32) * share[:, 32 + h:33 + h] for h in range(NH)]
        for h in range(NH):
            for k in (1, 3, 2):
                arrived(precv.at[h, half, back(v, k)], pp_s.at[h, half, k], pp_r.at[h, half, k])
            for j in range(4):
                heads[h] += precv[h, half, j].astype(F32) * share[:, j * 8 + h:j * 8 + h + 1]
        attended = jnp.concatenate(heads, axis=1).astype(BF16)
        for n in range(NC):
            c = slice(n * CW, (n + 1) * CW)
            proj = jnp.dot(attended, wv[:, c], preferred_element_type=F32)
            ys[half, :, :, c] = proj.reshape(4, 8, CW).astype(BF16)
            for k in (2, 1, 3):
                to = lax.rem(y + k, 4)
                send(ys.at[half, to, :, c], yr.at[half, y, :, c], y_s.at[half, n, k], y_r.at[half, n, k], p, at_y(k))

    for c in sends[:-2 * 3 * NC]:
        c.wait_send()
    del sends[:-2 * 3 * NC]

    def sum_y(half, n):
        c = slice(n * CW, (n + 1) * CW)
        a = ys[half, y, :, c].astype(F32)
        for k in (1, 3, 2):
            src = lax.rem(y + 4 - k, 4)
            arrived(yr.at[half, src, :, c], y_s.at[half, n, k], y_r.at[half, n, k])
            a += yr[half, src, :, c].astype(F32)
        return a

    for n in range(NC):
        c = slice(n * CW, (n + 1) * CW)
        zs[:, c] = sum_y(1, n).astype(BF16)
        send(zs.at[:, c], zr.at[:, c], z_s.at[n], z_r.at[n], p_w, other + y)

    slot = hd * 8 + lax.broadcasted_iota(jnp.int32, (8, 1), 0)
    live = slot < counts[p]
    halves = [sum_y(0, n) for n in range(NC)]
    for n in range(NC):
        c = slice(n * CW, (n + 1) * CW)
        arrived(zr.at[:, c], z_s.at[n], z_r.at[n])
        whole = halves[n] + zr[:, c].astype(F32) + bias[:, c]
        out[:, c] = jnp.where(live, gate[:, c] * whole, 0.0).astype(BF16)

    for c in sends:
        c.wait_send()


def on_device(queries, keys, values, stale_keys, stale_values, patch_counts, out_weight, out_bias, gate_scale):
    dma = pltpu.SemaphoreType.DMA
    vm = pltpu.VMEM
    hbm = pl.BlockSpec(memory_space=pltpu.HBM)
    vmem = pl.BlockSpec(memory_space=pltpu.VMEM)

    def pair(*shape):
        return [dma(shape), dma(shape)]

    return pl.pallas_call(
        kernel,
        out_shape=pltpu.VMEM((8, D), BF16),
        in_specs=[hbm] * 9,
        out_specs=vmem,
        scratch_shapes=[
            pltpu.SMEM((64,), jnp.int32),
            vm((1, D), F32),
            vm((1, D), F32),
            vm((8, D), BF16),
            vm((8, D), BF16),
            vm((8, D), BF16),
            vm((4, 2, 4, 8, W3), BF16),
            vm((2, 4, 2, ROWS, W3), BF16),
            vm((4, 2, ROWS, W3), BF16),
            vm((NH, 4, 2, ROWS, HD), BF16),
            vm((2, 2, 2, 4, 8, W3), BF16),
            vm((W3, D), BF16),
            vm((2, QS, KEYS), F32),
            vm((NH, QS, HD), F32),
            vm((NH, QS, KEYS), BF16),
            vm((NH, 2, 4, 32, HD), BF16),
            vm((NH, 2, 4, 32, HD), BF16),
            vm((4, 16, HD), F32),
            vm((4, 16, HD), F32),
            vm((2, 4, 8, D), BF16),
            vm((2, 4, 8, D), BF16),
            vm((8, D), BF16),
            vm((8, D), BF16),
            dma((12,)),
            *pair(2, 4),
            *pair(2, 2, 4),
            *pair(2, 4),
            *pair(3, 4),
            *pair(NH + 1),
            *pair(3, 4),
            *pair(NH, 4, 2),
            *pair(2, 2),
            *pair(NH, 2, 4),
            *pair(4),
            *pair(2, NC, 4),
            *pair(NC),
        ],
        compiler_params=pltpu.CompilerParams(collective_id=0, has_side_effects=True, vmem_limit_bytes=60 * 2**20),
        cost_estimate=pl.CostEstimate(flops=600_000_000, bytes_accessed=3_000_000, transcendentals=800_000),
    )(patch_counts, queries, keys, values, stale_keys, stale_values, out_weight, out_bias.reshape(1, D), gate_scale.reshape(1, D))


def solution(mesh):
    in_specs = (
        P(("patch", "head"), None),
        P(("patch", "head"), None),
        P(("patch", "head"), None),
        P("patch", "head"),
        P("patch", "head"),
        P(),
        P("head", None),
        P(),
        P(),
    )
    return jax.shard_map(on_device, mesh=mesh, in_specs=in_specs, out_specs=P(("patch", "head"), None), check_vma=False)
```
